256 devices in a mesh: grp: 8 (over z), brick: 32 (over x, y, core).
Axes of the slice: x: 4, y: 4, z: 8, core: 2. Of those that a mesh axis runs over, the one named last changes fastest.
Arguments:
- store: bfloat16 [768, 256, 256], P(('grp', 'brick')), may hold values from -0.005859375 to 0.005859375
- crossing: int32 [256, 16], P('grp'), may hold values from 0 to 95, as said below
- phi: bfloat16 [64, 256, 16, 1024], P('grp', 'brick'), may hold values from -6 to 6
- rows_index: int32 [256, 16, 256], P(('grp', 'brick')), may hold values from 0 to 1023
- cols_index: int32 [256, 16, 256], P(('grp', 'brick')), may hold values from 0 to 1023
Outputs:
- hamiltonian: float32 [768, 256, 256], P(('grp', 'brick'))
The draws below stay inside these ranges and needn't reach their ends.
Inputs may be any that keep to these rules, and one draw needn't show every extreme that they name: `crossing`: each row lists 16 different blocks of its group; block k of a group is held by the device with brick index k // 3 of that group. A row names at most 1 block held by one device, and exactly 1 of some device.
All inputs are finite; a program needn't handle non-finite values.
Results may differ from the reference program's by a relative error of at most 0.0029.
Values may be sent and summed in bfloat16 or wider, within the bound.
No kernel may reach another device: no remote copies, remote signals or barrier semaphores. Data moves between devices by JAX's collectives and lax.ppermute only.
A program may use at most 128 MiB of HBM per device.

```python
import math
import jax
import jax.numpy as jnp
from jax import lax

NF = 256
F = 1024
CAP = 1
OWN = 3
CX = 8
CY = 8
CZ = 16
NBLK = 16
BRICKS = 256
NX = 64
NY = 256
N_GRP = 8
N_BRICK = 32


def draw_crossing(key, part):

    def single_row(row_key):
        key_order, key_first, key_offset = jax.random.split(row_key, 3)
        items = N_BRICK * CAP
        position = jax.random.permutation(key_order, items).astype(jnp.int32)
        owner = jnp.arange(items, dtype=jnp.int32) // CAP
        first = jax.random.randint(key_first, (), 0, N_BRICK, dtype=jnp.int32)
        score = jnp.where(owner == first, -1, position)
        order = jnp.argsort(score, stable=True)[:NBLK].astype(jnp.int32)
        offsets = jax.random.randint(key_offset, (N_BRICK,), 0, OWN, dtype=jnp.int32)
        chosen_owner = order // CAP
        chosen_slot = order % CAP
        return (chosen_owner * OWN + (offsets[chosen_owner] + chosen_slot * (OWN // CAP)) % OWN).astype(jnp.int32)
    return jax.vmap(single_row)(jax.random.split(key, N_GRP * N_BRICK))


def set_ends(entries, own_key, low, high):
    dims = entries.shape
    spot = [jax.random.randint(jax.random.fold_in(own_key, axis), (), 0, dims[axis]) for axis in range(len(dims))]
    entries = entries.at[tuple(spot)].set(low)
    longest = dims.index(max(dims))
    spot[longest] = (spot[longest] + 1) % dims[longest]
    return entries.at[tuple(spot)].set(high)


def block_scale(own_key, shape, cuts, low, largest):
    level, own = 1.0, jax.random.fold_in(own_key, 6)
    for dim, parts in cuts:
        heights = jnp.exp(jax.random.uniform(jax.random.fold_in(own, dim), (parts,), jnp.float32, low / len(cuts), largest / len(cuts)))
        level = level * jnp.repeat(heights, shape[dim] // parts).reshape([-1 if axis == dim else 1 for axis in range(len(shape))])
    return level


def bell_draw(own_key, extent, scale, bound, cuts=(), kind=jnp.bfloat16):
    loudness = block_scale(own_key, extent, cuts, -0.22, 0.18) if cuts else 1.0
    array = jax.random.normal(own_key, extent, jnp.float32) * scale * loudness
    return jnp.minimum(jnp.maximum(array, -bound), bound).astype(kind)


def setup_inputs(seed: int = 0) -> dict:
    key_list = jax.random.split(jax.random.key(seed), 6)
    store = bell_draw(key_list[0], (BRICKS * OWN, NF, NF), (NBLK * NF * NF) ** -0.5, 0.005859375, ((0, 256),))
    crossing = draw_crossing(jax.random.fold_in(key_list[5], 71), 0)
    phi = bell_draw(key_list[2], (NX, NY, CZ, F), 1.0, 6.0, ((0, 8), (1, 32)))
    rows_index = set_ends(jax.random.randint(key_list[3], (BRICKS, NBLK, NF), 0, F), jax.random.fold_in(key_list[3], 1), 0, F - 1).astype(jnp.int32)
    cols_index = set_ends(jax.random.randint(key_list[4], (BRICKS, NBLK, NF), 0, F), jax.random.fold_in(key_list[4], 1), 0, F - 1).astype(jnp.int32)
    return {"store": store, "crossing": crossing, "phi": phi, "rows_index": rows_index, "cols_index": cols_index}


GRAD_WEIGHT = 0.5

def brick_table(phi, brick_id):
    group = brick_id // N_BRICK
    member = brick_id % N_BRICK
    zero = jnp.zeros((), jnp.int32)
    piece = lax.dynamic_slice(phi, ((group * CX).astype(jnp.int32), (member * CY).astype(jnp.int32), zero, zero), (CX, CY, CZ, F))
    return piece.reshape(CX * CY * CZ, F).T

def difference(field, axis):
    return (jnp.roll(field, -1, axis) - jnp.roll(field, 1, axis)) * 0.5

def potential_of(density):
    grad_x = difference(density, 0)
    grad_y = difference(density, 1)
    grad_z = difference(density, 2)
    sigma = grad_x * grad_x + grad_y * grad_y + grad_z * grad_z
    factor = 2.0 * GRAD_WEIGHT / (1.0 + sigma)
    diverge = difference(factor * grad_x, 0) + difference(factor * grad_y, 1) + difference(factor * grad_z, 2)
    return density / jnp.sqrt(1.0 + density * density) - diverge

def reference(store, crossing, phi, rows_index, cols_index):
    points = CX * CY * CZ
    dvol = 1.0 / math.sqrt(points)
    block_ids = jnp.arange(NBLK, dtype=jnp.int32)

    def global_ids(brick_id):
        return (brick_id // N_BRICK * (N_BRICK * OWN) + crossing[brick_id]).astype(jnp.int32)

    def collocate(brick_id):
        table = brick_table(phi, brick_id)
        ids = global_ids(brick_id)

        def single(index):
            left = table[rows_index[brick_id, index]]
            right = table[cols_index[brick_id, index]]
            product = jnp.dot(store[ids[index]], right, preferred_element_type=jnp.float32)
            return lax.optimization_barrier(jnp.sum(left.astype(jnp.float32) * product, axis=0))
        return lax.optimization_barrier(jnp.sum(lax.map(single, block_ids), axis=0))
    bricks_all = jnp.arange(N_GRP * N_BRICK, dtype=jnp.int32)
    dens = lax.map(collocate, bricks_all)
    density = dens.reshape(N_GRP, N_BRICK, CX, CY, CZ).transpose(0, 2, 1, 3, 4).reshape(N_GRP * CX, N_BRICK * CY, CZ)
    potential = potential_of(density)
    pot_bricks = potential.reshape(N_GRP, CX, N_BRICK, CY, CZ).transpose(0, 2, 1, 3, 4).reshape(N_GRP * N_BRICK, points)

    def integrate(total, brick_id):
        table = brick_table(phi, brick_id)
        ids = global_ids(brick_id)
        scaled = pot_bricks[brick_id] * dvol

        def single(index):
            left = table[rows_index[brick_id, index]]
            weighted = (table[cols_index[brick_id, index]].astype(jnp.float32) * scaled[None, :]).astype(jnp.bfloat16)
            return lax.dot_general(left, weighted, (((1,), (1,)), ((), ())), preferred_element_type=jnp.float32)
        partial_value = lax.map(single, block_ids)
        return (total.at[ids].add(partial_value), None)
    start = jnp.zeros((N_GRP * N_BRICK * OWN, NF, NF), jnp.float32)
    hamiltonian, unused = lax.scan(integrate, start, bricks_all)
    return hamiltonian
```

```python
import math

import jax
import jax.numpy as jnp
from jax import lax
from jax.experimental import pallas as pl
from jax.experimental.pallas import tpu as pltpu
from jax.sharding import PartitionSpec as P

GRAD_WEIGHT = 0.5
MIB = 1024 * 1024


def params(mib=40):
    return pltpu.CompilerParams(vmem_limit_bytes=mib * MIB)


def pick_blocks(ids, store, group=4):
    count = ids.shape[0]
    own, rows, cols = store.shape

    def kernel(ids_ref, store_ref, out_ref):
        base = pl.program_id(0) * group
        for i in range(group):
            out_ref[i] = store_ref[ids_ref[base + i]]

    return pl.pallas_call(
        kernel,
        out_shape=jax.ShapeDtypeStruct((count, rows, cols), store.dtype),
        grid_spec=pltpu.PrefetchScalarGridSpec(
            num_scalar_prefetch=1,
            grid=(count // group,),
            in_specs=[pl.BlockSpec((own, rows, cols), lambda i, ids: (0, 0, 0))],
            out_specs=pl.BlockSpec((group, rows, cols), lambda i, ids: (i, 0, 0)),
        ),
        compiler_params=params(),
        name="pick_blocks",
    )(ids, store)


def gather_tables(index, table):
    count, _, width = index.shape
    functions, points = table.shape
    lanes = 128

    def kernel(index_ref, table_ref, out_ref):
        pieces = []
        for start in range(0, width, lanes):
            row = index_ref[0, :, start : start + lanes]
            column = jnp.broadcast_to(row, (lanes, lanes)).T
            hot = [
                jnp.where(
                    column == lax.broadcasted_iota(jnp.int32, (lanes, lanes), 1) + f, 1.0, 0.0
                ).astype(jnp.bfloat16)
                for f in range(0, functions, lanes)
            ]
            pieces.append(jnp.concatenate(hot, axis=1))
        onehot = jnp.concatenate(pieces, axis=0)
        out_ref[0] = jnp.dot(
            onehot, table_ref[...], preferred_element_type=jnp.float32
        ).astype(jnp.bfloat16)

    return pl.pallas_call(
        kernel,
        out_shape=jax.ShapeDtypeStruct((count, width, points), jnp.bfloat16),
        grid=(count,),
        in_specs=[
            pl.BlockSpec((1, 1, width), lambda i: (i, 0, 0)),
            pl.BlockSpec((functions, points), lambda i: (0, 0)),
        ],
        out_specs=pl.BlockSpec((1, width, points), lambda i: (i, 0, 0)),
        compiler_params=params(),
        cost_estimate=pl.CostEstimate(
            flops=2 * count * width * functions * points,
            bytes_accessed=2 * count * width * points,
            transcendentals=0,
        ),
        name="gather_tables",
    )(index, table)


def collocate(slots, blocks, tables):
    count, both, points = tables.shape
    width = both // 2

    def kernel(slots_ref, block_ref, table_ref, out_ref):
        @pl.when(pl.program_id(0) == 0)
        def _():
            out_ref[...] = jnp.zeros_like(out_ref)

        product = jnp.dot(
            block_ref[0], table_ref[0, width:, :], preferred_element_type=jnp.float32
        )
        term = table_ref[0, :width, :].astype(jnp.float32) * product
        out_ref[...] += jnp.sum(term.reshape(width // 8, 8, points), axis=0)

    return pl.pallas_call(
        kernel,
        out_shape=jax.ShapeDtypeStruct((8, points), jnp.float32),
        grid_spec=pltpu.PrefetchScalarGridSpec(
            num_scalar_prefetch=1,
            grid=(count,),
            in_specs=[
                pl.BlockSpec((1, width, width), lambda j, slots: (slots[j], 0, 0)),
                pl.BlockSpec((1, both, points), lambda j, slots: (j, 0, 0)),
            ],
            out_specs=pl.BlockSpec((8, points), lambda j, slots: (0, 0)),
        ),
        compiler_params=params(),
        name="collocate",
    )(slots, blocks, tables)


def integrate(slots, scaled, tables, total):
    count, both, points = tables.shape
    width = both // 2

    def kernel(slots_ref, scaled_ref, table_ref, out_ref):
        weighted = (table_ref[0, width:, :].astype(jnp.float32) * scaled_ref[...]).astype(
            jnp.bfloat16
        )
        out_ref[0] = lax.dot_general(
            table_ref[0, :width, :],
            weighted,
            (((1,), (1,)), ((), ())),
            preferred_element_type=jnp.float32,
        ).astype(jnp.bfloat16)

    return pl.pallas_call(
        kernel,
        out_shape=jax.ShapeDtypeStruct((total, width, width), jnp.bfloat16),
        grid_spec=pltpu.PrefetchScalarGridSpec(
            num_scalar_prefetch=1,
            grid=(count,),
            in_specs=[
                pl.BlockSpec((1, points), lambda j, slots: (0, 0)),
                pl.BlockSpec((1, both, points), lambda j, slots: (j, 0, 0)),
            ],
            out_specs=pl.BlockSpec((1, width, width), lambda j, slots: (slots[j], 0, 0)),
        ),
        compiler_params=params(),
        name="integrate",
    )(slots, scaled, tables)


def add_up(targets, parts, own_count, group=8):
    count, rows, cols = parts.shape

    def kernel(targets_ref, parts_ref, out_ref):
        step = pl.program_id(0)

        @pl.when(step == 0)
        def _():
            out_ref[...] = jnp.zeros_like(out_ref)

        for i in range(group):
            target = targets_ref[step * group + i]

            @pl.when(target >= 0)
            def _():
                out_ref[target] += parts_ref[i].astype(jnp.float32)

    return pl.pallas_call(
        kernel,
        out_shape=jax.ShapeDtypeStruct((own_count, rows, cols), jnp.float32),
        grid_spec=pltpu.PrefetchScalarGridSpec(
            num_scalar_prefetch=1,
            grid=(count // group,),
            in_specs=[pl.BlockSpec((group, rows, cols), lambda i, t: (i, 0, 0))],
            out_specs=pl.BlockSpec((own_count, rows, cols), lambda i, t: (0, 0, 0)),
        ),
        compiler_params=params(),
        name="add_up",
    )(targets, parts)


def extended(block, axis, dim, width):
    count = lax.axis_size(axis)
    forward = [(i, (i + 1) % count) for i in range(count)]
    backward = [(target, source) for source, target in forward]
    size = block.shape[dim]
    low = lax.ppermute(lax.slice_in_dim(block, size - width, size, axis=dim), axis, forward)
    high = lax.ppermute(lax.slice_in_dim(block, 0, width, axis=dim), axis, backward)
    return jnp.concatenate([low, block, high], axis=dim)


def middle(field, dim, width=1):
    return lax.slice_in_dim(field, width, field.shape[dim] - width, axis=dim)


def slope(field, dim):
    size = field.shape[dim]
    return (
        lax.slice_in_dim(field, 2, size, axis=dim) - lax.slice_in_dim(field, 0, size - 2, axis=dim)
    ) * 0.5


def slope_z(field):
    return (jnp.roll(field, -1, 2) - jnp.roll(field, 1, 2)) * 0.5


def potential_of(padded):
    grad_x = middle(slope(padded, 0), 1)
    grad_y = middle(slope(padded, 1), 0)
    centre = middle(middle(padded, 0), 1)
    grad_z = slope_z(centre)
    sigma = grad_x * grad_x + grad_y * grad_y + grad_z * grad_z
    factor = 2.0 * GRAD_WEIGHT / (1.0 + sigma)
    flux_z = middle(middle(factor * grad_z, 0), 1)
    diverge = (
        middle(slope(factor * grad_x, 0), 1) + middle(slope(factor * grad_y, 1), 0) + slope_z(flux_z)
    )
    density = middle(middle(centre, 0), 1)
    return density / jnp.sqrt(1.0 + density * density) - diverge


def local(store, crossing, phi, rows_index, cols_index):
    position = lax.axis_index("brick")
    brick_count = lax.axis_size("brick")
    own_count, width = store.shape[0], store.shape[1]
    size_x, size_y, size_z, functions = phi.shape
    points = size_x * size_y * size_z
    owners = crossing // own_count
    chosen = owners == position
    filled = jnp.any(chosen, axis=-1)
    send_ids = jnp.sum(jnp.where(chosen, crossing % own_count, 0), axis=-1)
    slots = lax.dynamic_index_in_dim(owners, position, 0, keepdims=False)

    sending = pick_blocks(send_ids, store)
    blocks = lax.all_to_all(sending, "brick", split_axis=0, concat_axis=0, tiled=True)
    table = phi.reshape(points, functions).T
    index = jnp.concatenate([rows_index[0], cols_index[0]], axis=1)[:, None, :]
    tables = gather_tables(index, table)
    density = jnp.sum(collocate(slots, blocks, tables), axis=0).reshape(size_x, size_y, size_z)
    padded = extended(extended(density, "grp", 0, 2), "brick", 1, 2)
    scaled = potential_of(padded).reshape(1, points) * (1.0 / math.sqrt(points))
    returning = integrate(slots, scaled, tables, brick_count)
    arrived = lax.all_to_all(returning, "brick", split_axis=0, concat_axis=0, tiled=True)
    targets = jnp.where(filled, send_ids, -1)
    return add_up(targets, arrived, own_count)


def solution(mesh):
    in_specs = (
        P(("grp", "brick"), None, None),
        P("grp", None),
        P("grp", "brick", None, None),
        P(("grp", "brick"), None, None),
        P(("grp", "brick"), None, None),
    )
    out_specs = P(("grp", "brick"), None, None)
    return jax.shard_map(local, mesh=mesh, in_specs=in_specs, out_specs=out_specs, check_vma=False)
```

```python
import math

import jax
import jax.numpy as jnp
from jax import lax
from jax.experimental import pallas as pl
from jax.experimental.pallas import tpu as pltpu
from jax.sharding import PartitionSpec as P

GRAD_WEIGHT = 0.5
MIB = 1024 * 1024


RESIDENT = pl.BlockSpec(memory_space=pltpu.VMEM)
IN_HBM = pl.BlockSpec(memory_space=pltpu.HBM)
SCALARS = pl.BlockSpec(memory_space=pltpu.SMEM)


def params(mib):
    return pltpu.CompilerParams(vmem_limit_bytes=mib * MIB)


def pick_blocks(ids, store):
    count = ids.shape[0]

    def kernel(ids_ref, store_ref, out_ref, sems):
        copies = [
            pltpu.make_async_copy(store_ref.at[ids_ref[i]], out_ref.at[i], sems.at[i])
            for i in range(count)
        ]
        for copy in copies:
            copy.start()
        for copy in copies:
            copy.wait()

    return pl.pallas_call(
        kernel,
        out_shape=pltpu.HBM((count,) + store.shape[1:], store.dtype),
        in_specs=[SCALARS, RESIDENT],
        out_specs=IN_HBM,
        scratch_shapes=[pltpu.SemaphoreType.DMA((count,))],
        compiler_params=params(4),
        name="pick_blocks",
    )(ids, store)


def gather_tables(index, table):
    count, _, width = index.shape
    functions, points = table.shape
    lanes = 128

    def kernel(index_ref, table_ref, out_ref):
        pieces = []
        for start in range(0, width, lanes):
            row = index_ref[0, :, start : start + lanes]
            column = jnp.broadcast_to(row, (lanes, lanes)).T
            hot = [
                jnp.where(
                    column == lax.broadcasted_iota(jnp.int32, (lanes, lanes), 1) + f, 1.0, 0.0
                ).astype(jnp.bfloat16)
                for f in range(0, functions, lanes)
            ]
            pieces.append(jnp.concatenate(hot, axis=1))
        onehot = jnp.concatenate(pieces, axis=0)
        out_ref[0] = jnp.dot(
            onehot, table_ref[...], preferred_element_type=jnp.float32
        ).astype(jnp.bfloat16)

    return pl.pallas_call(
        kernel,
        out_shape=pltpu.HBM((count, width, points), jnp.bfloat16),
        grid=(count,),
        in_specs=[
            pl.BlockSpec((1, 1, width), lambda i: (i, 0, 0)),
            pl.BlockSpec((functions, points), lambda i: (0, 0)),
        ],
        out_specs=pl.BlockSpec((1, width, points), lambda i: (i, 0, 0)),
        compiler_params=params(24),
        cost_estimate=pl.CostEstimate(
            flops=2 * count * width * functions * points,
            bytes_accessed=2 * count * width * points,
            transcendentals=0,
        ),
        name="gather_tables",
    )(index, table)


def collocate(slots, blocks, tables):
    count, both, points = tables.shape
    width = both // 2

    def kernel(slots_ref, blocks_ref, tables_ref, out_ref, held, kept, sems):
        def fetch(j):
            return (
                pltpu.make_async_copy(blocks_ref.at[slots_ref[j]], held.at[j], sems.at[0, j]),
                pltpu.make_async_copy(tables_ref.at[j], kept.at[j], sems.at[1, j]),
            )

        for j in range(count):
            for copy in fetch(j):
                copy.start()
        out_ref[...] = jnp.zeros_like(out_ref)

        def body(j, carry):
            for copy in fetch(j):
                copy.wait()
            product = jnp.dot(held[j], kept[j, width:, :], preferred_element_type=jnp.float32)
            term = kept[j, :width, :].astype(jnp.float32) * product
            out_ref[...] += jnp.sum(term.reshape(width // 8, 8, points), axis=0)
            return carry

        lax.fori_loop(0, count, body, 0)

    return pl.pallas_call(
        kernel,
        out_shape=jax.ShapeDtypeStruct((8, points), jnp.float32),
        in_specs=[SCALARS, IN_HBM, IN_HBM],
        out_specs=RESIDENT,
        scratch_shapes=[
            pltpu.VMEM((count, width, width), jnp.bfloat16),
            pltpu.VMEM(tables.shape, tables.dtype),
            pltpu.SemaphoreType.DMA((2, count)),
        ],
        compiler_params=params(52),
        name="collocate",
    )(slots, blocks, tables)


def integrate(slots, scaled, tables, total):
    count, both, points = tables.shape
    width = both // 2

    def kernel(slots_ref, scaled_ref, tables_ref, out_ref, held, kept, sems):
        def fetch(j):
            return pltpu.make_async_copy(tables_ref.at[j], kept.at[j], sems.at[1, j])

        def leave(j):
            return pltpu.make_async_copy(held.at[j], out_ref.at[slots_ref[j]], sems.at[0, j])

        for j in range(count):
            fetch(j).start()

        def body(j, carry):
            fetch(j).wait()
            weighted = (kept[j, width:, :].astype(jnp.float32) * scaled_ref[...]).astype(
                jnp.bfloat16
            )
            held[j] = lax.dot_general(
                kept[j, :width, :],
                weighted,
                (((1,), (1,)), ((), ())),
                preferred_element_type=jnp.float32,
            ).astype(jnp.bfloat16)
            leave(j).start()
            return carry

        lax.fori_loop(0, count, body, 0)
        for j in range(count):
            leave(j).wait()

    return pl.pallas_call(
        kernel,
        out_shape=pltpu.HBM((total, width, width), jnp.bfloat16),
        in_specs=[SCALARS, RESIDENT, IN_HBM],
        out_specs=IN_HBM,
        scratch_shapes=[
            pltpu.VMEM((count, width, width), jnp.bfloat16),
            pltpu.VMEM(tables.shape, tables.dtype),
            pltpu.SemaphoreType.DMA((2, count)),
        ],
        compiler_params=params(52),
        name="integrate",
    )(slots, scaled, tables)


def add_up(targets, parts, own_count):
    count, rows, cols = parts.shape

    def kernel(targets_ref, parts_ref, out_ref, held, sems):
        def fetch(i):
            return pltpu.make_async_copy(parts_ref.at[i], held.at[i], sems.at[i])

        for i in range(count):

            @pl.when(targets_ref[i] >= 0)
            def _():
                fetch(i).start()

        out_ref[...] = jnp.zeros_like(out_ref)
        for i in range(count):
            target = targets_ref[i]

            @pl.when(target >= 0)
            def _():
                fetch(i).wait()
                out_ref[target] += held[i].astype(jnp.float32)

    return pl.pallas_call(
        kernel,
        out_shape=jax.ShapeDtypeStruct((own_count, rows, cols), jnp.float32),
        in_specs=[SCALARS, IN_HBM],
        out_specs=RESIDENT,
        scratch_shapes=[
            pltpu.VMEM((count, rows, cols), parts.dtype),
            pltpu.SemaphoreType.DMA((count,)),
        ],
        compiler_params=params(12),
        name="add_up",
    )(targets, parts)


def ends(block, dim, width):
    size = block.shape[dim]
    return (
        lax.slice_in_dim(block, 0, width, axis=dim),
        lax.slice_in_dim(block, size - width, size, axis=dim),
    )


def extended_ring(block, axis, dim, width):
    count = lax.axis_size(axis)
    low, high = ends(block, dim, width)
    forward = [(i, (i + 1) % count) for i in range(count)]
    backward = [(target, source) for source, target in forward]
    below = lax.ppermute(high, axis, forward)
    above = lax.ppermute(low, axis, backward)
    return jnp.concatenate([below, block, above], axis=dim)


def extended_pairs(block, axis, dim, width):
    count = lax.axis_size(axis)
    odd = lax.axis_index(axis) % 2 == 1
    low, high = ends(block, dim, width)
    within = [(i, i ^ 1) for i in range(count)]
    between = [(i, (i + 1) % count if i % 2 else (i - 1) % count) for i in range(count)]
    far = lax.ppermute(jnp.where(odd, high, low), axis, between)
    near = lax.ppermute(jnp.where(odd, low, high), axis, within)
    below = jnp.where(odd, near, far)
    above = jnp.where(odd, far, near)
    return jnp.concatenate([below, block, above], axis=dim)


def middle(field, dim, width=1):
    return lax.slice_in_dim(field, width, field.shape[dim] - width, axis=dim)


def slope(field, dim):
    size = field.shape[dim]
    return (
        lax.slice_in_dim(field, 2, size, axis=dim) - lax.slice_in_dim(field, 0, size - 2, axis=dim)
    ) * 0.5


def slope_z(field):
    return (jnp.roll(field, -1, 2) - jnp.roll(field, 1, 2)) * 0.5


def potential_of(padded):
    grad_x = middle(slope(padded, 0), 1)
    grad_y = middle(slope(padded, 1), 0)
    centre = middle(middle(padded, 0), 1)
    grad_z = slope_z(centre)
    sigma = grad_x * grad_x + grad_y * grad_y + grad_z * grad_z
    factor = 2.0 * GRAD_WEIGHT / (1.0 + sigma)
    flux_z = middle(middle(factor * grad_z, 0), 1)
    diverge = (
        middle(slope(factor * grad_x, 0), 1) + middle(slope(factor * grad_y, 1), 0) + slope_z(flux_z)
    )
    density = middle(middle(centre, 0), 1)
    return density / jnp.sqrt(1.0 + density * density) - diverge


def local(store, crossing, phi, rows_index, cols_index):
    position = lax.axis_index("brick")
    brick_count = lax.axis_size("brick")
    own_count, width = store.shape[0], store.shape[1]
    size_x, size_y, size_z, functions = phi.shape
    points = size_x * size_y * size_z
    owners = crossing // own_count
    chosen = owners == position
    filled = jnp.any(chosen, axis=-1)
    send_ids = jnp.sum(jnp.where(chosen, crossing % own_count, 0), axis=-1)
    slots = lax.dynamic_index_in_dim(owners, position, 0, keepdims=False)

    sending = pick_blocks(send_ids, store)
    blocks = lax.all_to_all(sending, "brick", split_axis=0, concat_axis=0, tiled=True)
    table = phi.reshape(points, functions).T
    index = jnp.concatenate([rows_index[0], cols_index[0]], axis=1)[:, None, :]
    tables = gather_tables(index, table)
    density = jnp.sum(collocate(slots, blocks, tables), axis=0).reshape(size_x, size_y, size_z)
    padded = extended_pairs(extended_ring(density, "grp", 0, 2), "brick", 1, 2)
    scaled = potential_of(padded).reshape(1, points) * (1.0 / math.sqrt(points))
    returning = integrate(slots, scaled, tables, brick_count)
    arrived = lax.all_to_all(returning, "brick", split_axis=0, concat_axis=0, tiled=True)
    targets = jnp.where(filled, send_ids, -1)
    return add_up(targets, arrived, own_count)


def solution(mesh):
    in_specs = (
        P(("grp", "brick"), None, None),
        P("grp", None),
        P("grp", "brick", None, None),
        P(("grp", "brick"), None, None),
        P(("grp", "brick"), None, None),
    )
    out_specs = P(("grp", "brick"), None, None)
    return jax.shard_map(local, mesh=mesh, in_specs=in_specs, out_specs=out_specs, check_vma=False)
```

```python
import math

import jax
import jax.numpy as jnp
from jax import lax
from jax.experimental import pallas as pl
from jax.experimental.pallas import tpu as pltpu
from jax.sharding import Mesh
from jax.sharding import PartitionSpec as P

GRAD_WEIGHT = 0.5
BRICK = ("x", "y", "core")
MIB = 1024 * 1024


RESIDENT = pl.BlockSpec(memory_space=pltpu.VMEM)
IN_HBM = pl.BlockSpec(memory_space=pltpu.HBM)
SCALARS = pl.BlockSpec(memory_space=pltpu.SMEM)


def params(mib):
    return pltpu.CompilerParams(vmem_limit_bytes=mib * MIB)


def pick_blocks(ids, store):
    count = ids.shape[0]

    def kernel(ids_ref, store_ref, out_ref, sems):
        copies = [
            pltpu.make_async_copy(store_ref.at[ids_ref[i]], out_ref.at[i], sems.at[i])
            for i in range(count)
        ]
        for copy in copies:
            copy.start()
        for copy in copies:
            copy.wait()

    return pl.pallas_call(
        kernel,
        out_shape=pltpu.HBM((count,) + store.shape[1:], store.dtype),
        in_specs=[SCALARS, RESIDENT],
        out_specs=IN_HBM,
        scratch_shapes=[pltpu.SemaphoreType.DMA((count,))],
        compiler_params=params(4),
        name="pick_blocks",
    )(ids, store)


def gather_tables(index, table):
    count, _, width = index.shape
    functions, points = table.shape
    lanes = 128

    def kernel(index_ref, table_ref, out_ref):
        pieces = []
        for start in range(0, width, lanes):
            row = index_ref[0, :, start : start + lanes]
            column = jnp.broadcast_to(row, (lanes, lanes)).T
            hot = [
                jnp.where(
                    column == lax.broadcasted_iota(jnp.int32, (lanes, lanes), 1) + f, 1.0, 0.0
                ).astype(jnp.bfloat16)
                for f in range(0, functions, lanes)
            ]
            pieces.append(jnp.concatenate(hot, axis=1))
        onehot = jnp.concatenate(pieces, axis=0)
        out_ref[0] = jnp.dot(
            onehot, table_ref[...], preferred_element_type=jnp.float32
        ).astype(jnp.bfloat16)

    return pl.pallas_call(
        kernel,
        out_shape=pltpu.HBM((count, width, points), jnp.bfloat16),
        grid=(count,),
        in_specs=[
            pl.BlockSpec((1, 1, width), lambda i: (i, 0, 0)),
            pl.BlockSpec((functions, points), lambda i: (0, 0)),
        ],
        out_specs=pl.BlockSpec((1, width, points), lambda i: (i, 0, 0)),
        compiler_params=params(24),
        cost_estimate=pl.CostEstimate(
            flops=2 * count * width * functions * points,
            bytes_accessed=2 * count * width * points,
            transcendentals=0,
        ),
        name="gather_tables",
    )(index, table)


def collocate(slots, blocks, tables):
    count, both, points = tables.shape
    width = both // 2

    def kernel(slots_ref, blocks_ref, tables_ref, out_ref, held, kept, sems):
        def fetch(j):
            return (
                pltpu.make_async_copy(blocks_ref.at[slots_ref[j]], held.at[j], sems.at[0, j]),
                pltpu.make_async_copy(tables_ref.at[j], kept.at[j], sems.at[1, j]),
            )

        for j in range(count):
            for copy in fetch(j):
                copy.start()
        out_ref[...] = jnp.zeros_like(out_ref)

        def body(j, carry):
            for copy in fetch(j):
                copy.wait()
            product = jnp.dot(held[j], kept[j, width:, :], preferred_element_type=jnp.float32)
            term = kept[j, :width, :].astype(jnp.float32) * product
            out_ref[...] += jnp.sum(term.reshape(width // 8, 8, points), axis=0)
            return carry

        lax.fori_loop(0, count, body, 0)

    return pl.pallas_call(
        kernel,
        out_shape=jax.ShapeDtypeStruct((8, points), jnp.float32),
        in_specs=[SCALARS, IN_HBM, IN_HBM],
        out_specs=RESIDENT,
        scratch_shapes=[
            pltpu.VMEM((count, width, width), jnp.bfloat16),
            pltpu.VMEM(tables.shape, tables.dtype),
            pltpu.SemaphoreType.DMA((2, count)),
        ],
        compiler_params=params(52),
        name="collocate",
    )(slots, blocks, tables)


def integrate(places, scaled, tables, total, half):
    count, both, points = tables.shape
    width = both // 2
    parts, inner = total

    def kernel(places_ref, scaled_ref, tables_ref, first_ref, *rest):
        others, (held, kept, sems) = rest[:parts], rest[parts:]

        def fetch(j):
            return pltpu.make_async_copy(tables_ref.at[j], kept.at[j], sems.at[0, j])

        def leave_first(j):
            return pltpu.make_async_copy(
                held.at[j, pl.ds(0, half)], first_ref.at[places_ref[0, j]], sems.at[1, j]
            )

        def leave_other(j, part):
            return pltpu.make_async_copy(
                held.at[j, pl.ds(half, width - half)],
                others[part].at[places_ref[2, j]],
                sems.at[2, j],
            )

        for j in range(count):
            fetch(j).start()

        def body(j, carry):
            fetch(j).wait()
            weighted = (kept[j, width:, :].astype(jnp.float32) * scaled_ref[...]).astype(
                jnp.bfloat16
            )
            held[j] = lax.dot_general(
                kept[j, :width, :],
                weighted,
                (((1,), (1,)), ((), ())),
                preferred_element_type=jnp.float32,
            ).astype(jnp.bfloat16)
            leave_first(j).start()
            for part in range(parts):

                @pl.when(places_ref[1, j] == part)
                def _():
                    leave_other(j, part).start()

            return carry

        lax.fori_loop(0, count, body, 0)
        for j in range(count):
            leave_first(j).wait()
            leave_other(j, 0).wait()

    return pl.pallas_call(
        kernel,
        out_shape=[pltpu.HBM((parts * inner, half, width), jnp.bfloat16)]
        + [pltpu.HBM((inner, width - half, width), jnp.bfloat16)] * parts,
        in_specs=[SCALARS, RESIDENT, IN_HBM],
        out_specs=[IN_HBM] * (1 + parts),
        scratch_shapes=[
            pltpu.VMEM((count, width, width), jnp.bfloat16),
            pltpu.VMEM(tables.shape, tables.dtype),
            pltpu.SemaphoreType.DMA((3, count)),
        ],
        compiler_params=params(52),
        name="integrate",
    )(places, scaled, tables)


def add_up(targets, parts, own_count, inner):
    rows, cols = parts[0].shape[1:]
    count = sum(part.shape[0] for part in parts)

    def kernel(targets_ref, *refs):
        parts_refs = refs[: len(parts)]
        own_ref, *outs = refs[len(parts) : len(parts) + inner]
        held, total, sems = refs[len(parts) + inner :]
        where = [(ref, i) for ref in parts_refs for i in range(ref.shape[0])]

        def fetch(i):
            ref, place = where[i]
            return pltpu.make_async_copy(ref.at[place], held.at[i], sems.at[i])

        for i in range(count):

            @pl.when(targets_ref[i] >= 0)
            def _():
                fetch(i).start()

        total[...] = jnp.zeros_like(total)
        for i in range(count):
            target = targets_ref[i]

            @pl.when(target >= 0)
            def _():
                fetch(i).wait()
                total[(i % inner) * own_count + target] += held[i].astype(jnp.float32)

        own_ref[...] = total[:own_count]
        for d, out in enumerate(outs):
            out[...] = total[(d + 1) * own_count : (d + 2) * own_count].astype(jnp.bfloat16)

    return pl.pallas_call(
        kernel,
        out_shape=[jax.ShapeDtypeStruct((own_count, rows, cols), jnp.float32)]
        + [jax.ShapeDtypeStruct((own_count, rows, cols), jnp.bfloat16)] * (inner - 1),
        in_specs=[SCALARS] + [IN_HBM] * len(parts),
        out_specs=[RESIDENT] * inner,
        scratch_shapes=[
            pltpu.VMEM((count, rows, cols), jnp.bfloat16),
            pltpu.VMEM((inner * own_count, rows, cols), jnp.float32),
            pltpu.SemaphoreType.DMA((count,)),
        ],
        compiler_params=params(12),
        name="add_up",
    )(targets, *parts)


def join(first, other):
    own_count, half, cols = first[0].shape
    rest = other[0].shape[1]

    def kernel(*refs):
        out_ref = refs[-1]

        def total(some):
            value = some[0][...]
            for ref in some[1:]:
                value = value + ref[...].astype(jnp.float32)
            return value

        out_ref[:, :half, :] = total(refs[: len(first)])
        out_ref[:, half:, :] = total(refs[len(first) : -1])

    return pl.pallas_call(
        kernel,
        out_shape=jax.ShapeDtypeStruct((own_count, half + rest, cols), jnp.float32),
        grid=(own_count,),
        in_specs=[pl.BlockSpec((1,) + a.shape[1:], lambda i: (i, 0, 0)) for a in first + other],
        out_specs=pl.BlockSpec((1, half + rest, cols), lambda i: (i, 0, 0)),
        compiler_params=params(8),
        name="join",
    )(*first, *other)


def ends(block, dim, width):
    size = block.shape[dim]
    return (
        lax.slice_in_dim(block, 0, width, axis=dim),
        lax.slice_in_dim(block, size - width, size, axis=dim),
    )


def extended_ring(block, axis, dim, width):
    count = lax.axis_size(axis)
    low, high = ends(block, dim, width)
    forward = [(i, (i + 1) % count) for i in range(count)]
    backward = [(target, source) for source, target in forward]
    below = lax.ppermute(high, axis, forward)
    above = lax.ppermute(low, axis, backward)
    return jnp.concatenate([below, block, above], axis=dim)


def extended_pairs(block, axis, dim, width):
    count = size_of(axis)
    odd = lax.axis_index(axis) % 2 == 1
    low, high = ends(block, dim, width)
    within = [(i, i ^ 1) for i in range(count)]
    between = [(i, (i + 1) % count if i % 2 else (i - 1) % count) for i in range(count)]
    far = lax.ppermute(jnp.where(odd, high, low), axis, between)
    near = lax.ppermute(jnp.where(odd, low, high), axis, within)
    below = jnp.where(odd, near, far)
    above = jnp.where(odd, far, near)
    return jnp.concatenate([below, block, above], axis=dim)


def middle(field, dim, width=1):
    return lax.slice_in_dim(field, width, field.shape[dim] - width, axis=dim)


def slope(field, dim):
    size = field.shape[dim]
    return (
        lax.slice_in_dim(field, 2, size, axis=dim) - lax.slice_in_dim(field, 0, size - 2, axis=dim)
    ) * 0.5


def slope_z(field):
    return (jnp.roll(field, -1, 2) - jnp.roll(field, 1, 2)) * 0.5


def potential_of(padded):
    grad_x = middle(slope(padded, 0), 1)
    grad_y = middle(slope(padded, 1), 0)
    centre = middle(middle(padded, 0), 1)
    grad_z = slope_z(centre)
    sigma = grad_x * grad_x + grad_y * grad_y + grad_z * grad_z
    factor = 2.0 * GRAD_WEIGHT / (1.0 + sigma)
    flux_z = middle(middle(factor * grad_z, 0), 1)
    diverge = (
        middle(slope(factor * grad_x, 0), 1) + middle(slope(factor * grad_y, 1), 0) + slope_z(flux_z)
    )
    density = middle(middle(centre, 0), 1)
    return density / jnp.sqrt(1.0 + density * density) - diverge


def size_of(axes):
    return math.prod(lax.axis_size(axis) for axis in axes)


def moved(value, dx=0, dy=0, dc=0):
    sizes = tuple(lax.axis_size(axis) for axis in BRICK)
    pairs = []
    for source in range(math.prod(sizes)):
        x, rest = divmod(source, sizes[1] * sizes[2])
        y, c = divmod(rest, sizes[2])
        x, y, c = (x + dx) % sizes[0], (y + dy) % sizes[1], (c + dc) % sizes[2]
        pairs.append((source, (x * sizes[1] + y) * sizes[2] + c))
    return lax.ppermute(value, BRICK, pairs)


def find(owners, ids, bricks, wanted):
    hit = owners[bricks][:, None, :] == wanted[None, :, None]
    number = jnp.sum(jnp.where(hit, ids[bricks][:, None, :], 0), axis=-1)
    return jnp.where(jnp.any(hit, axis=-1), number, -1).reshape(-1).astype(jnp.int32)


def local(store, crossing, phi, rows_index, cols_index):
    nx, ny, nc = (lax.axis_size(axis) for axis in BRICK)
    x, y, c = (lax.axis_index(axis) for axis in BRICK)
    position = (x * ny + y) * nc + c
    own_count, width = store.shape[0], store.shape[1]
    half = width // 2
    size_x, size_y, size_z, functions = phi.shape
    points = size_x * size_y * size_z
    owners = crossing // own_count
    ids = crossing % own_count
    chosen = owners == position
    send_ids = jnp.sum(jnp.where(chosen, ids, 0), axis=-1)
    slots = lax.dynamic_index_in_dim(owners, position, 0, keepdims=False)

    sending = pick_blocks(send_ids, store)
    blocks = lax.all_to_all(sending, BRICK, split_axis=0, concat_axis=0, tiled=True)
    table = phi.reshape(points, functions).T
    index = jnp.concatenate([rows_index[0], cols_index[0]], axis=1)[:, None, :]
    tables = gather_tables(index, table)
    density = jnp.sum(collocate(slots, blocks, tables), axis=0).reshape(size_x, size_y, size_z)
    padded = extended_pairs(extended_ring(density, "grp", 0, 2), BRICK, 1, 2)
    scaled = potential_of(padded).reshape(1, points) * (1.0 / math.sqrt(points))

    to_x, rest = slots // (ny * nc), slots % (ny * nc)
    to_y, to_c = rest // nc, rest % nc
    ahead_x, ahead_y, ahead_c = (to_x - x) % nx, (to_y - y) % ny, (to_c - c) % nc
    places = jnp.stack(
        [(to_y * nc + to_c) * nx + ahead_x, ahead_x * nc + ahead_c, ahead_y]
    ).astype(jnp.int32)
    first, *others = integrate(places, scaled, tables, (nx * nc, ny), half)
    first = lax.all_to_all(first, ("y", "core"), split_axis=0, concat_axis=0, tiled=True)
    others = [
        moved(piece, dx=i // nc, dc=i % nc) if i else piece for i, piece in enumerate(others)
    ]
    step_x, step_y, step_c = jnp.arange(nx), jnp.arange(ny), jnp.arange(nc)
    from_first = ((x * ny + step_y[:, None]) * nc + step_c[None, :]).reshape(-1)
    for_first = (((x + step_x) % nx) * ny + y) * nc + c
    from_other = (
        (((x - step_x) % nx) * ny + y)[:, None] * nc + ((c - step_c) % nc)[None, :]
    ).reshape(-1)
    for_other = (x * ny + (y + step_y) % ny) * nc + c
    other_own, *other_send = add_up(
        find(owners, ids, from_other, for_other), others, own_count, ny
    )
    other_all = [other_own] + [moved(piece, dy=1 + d) for d, piece in enumerate(other_send)]
    first_own, *first_send = add_up(
        find(owners, ids, from_first, for_first), [first], own_count, nx
    )
    first_all = [first_own] + [moved(piece, dx=1 + d) for d, piece in enumerate(first_send)]
    return join(first_all, other_all)


def solution(mesh):
    groups, bricks = mesh.shape["grp"], mesh.shape["brick"]
    side = math.isqrt(bricks // 2)
    split = Mesh(mesh.devices.reshape(groups, side, bricks // (2 * side), 2), ("grp",) + BRICK)
    whole = ("grp",) + BRICK
    in_specs = (
        P(whole, None, None),
        P("grp", None),
        P("grp", BRICK, None, None),
        P(whole, None, None),
        P(whole, None, None),
    )
    return jax.shard_map(
        local, mesh=split, in_specs=in_specs, out_specs=P(whole, None, None), check_vma=False
    )
```

```python
import math

import jax
import jax.numpy as jnp
from jax import lax
from jax.experimental import pallas as pl
from jax.experimental.pallas import tpu as pltpu
from jax.sharding import Mesh
from jax.sharding import PartitionSpec as P

GRAD_WEIGHT = 0.5
BRICK = ("x", "y", "core")
MIB = 1024 * 1024


RESIDENT = pl.BlockSpec(memory_space=pltpu.VMEM)
IN_HBM = pl.BlockSpec(memory_space=pltpu.HBM)
SCALARS = pl.BlockSpec(memory_space=pltpu.SMEM)


def params(mib):
    return pltpu.CompilerParams(vmem_limit_bytes=mib * MIB)


def pick_blocks(ids, store):
    count = ids.shape[0]

    def kernel(ids_ref, store_ref, out_ref, sems):
        copies = [
            pltpu.make_async_copy(store_ref.at[ids_ref[i]], out_ref.at[i], sems.at[i])
            for i in range(count)
        ]
        for copy in copies:
            copy.start()
        for copy in copies:
            copy.wait()

    return pl.pallas_call(
        kernel,
        out_shape=pltpu.HBM((count,) + store.shape[1:], store.dtype),
        in_specs=[SCALARS, RESIDENT],
        out_specs=IN_HBM,
        scratch_shapes=[pltpu.SemaphoreType.DMA((count,))],
        compiler_params=params(4),
        name="pick_blocks",
    )(ids, store)


def gather_tables(index, table):
    count, _, width = index.shape
    functions, points = table.shape
    lanes = 128

    def kernel(index_ref, table_ref, out_ref):
        pieces = []
        for start in range(0, width, lanes):
            row = index_ref[0, :, start : start + lanes]
            column = jnp.broadcast_to(row, (lanes, lanes)).T
            hot = [
                jnp.where(
                    column == lax.broadcasted_iota(jnp.int32, (lanes, lanes), 1) + f, 1.0, 0.0
                ).astype(jnp.bfloat16)
                for f in range(0, functions, lanes)
            ]
            pieces.append(jnp.concatenate(hot, axis=1))
        onehot = jnp.concatenate(pieces, axis=0)
        out_ref[0] = jnp.dot(
            onehot, table_ref[...], preferred_element_type=jnp.float32
        ).astype(jnp.bfloat16)

    return pl.pallas_call(
        kernel,
        out_shape=pltpu.HBM((count, width, points), jnp.bfloat16),
        grid=(count,),
        in_specs=[
            pl.BlockSpec((1, 1, width), lambda i: (i, 0, 0)),
            pl.BlockSpec((functions, points), lambda i: (0, 0)),
        ],
        out_specs=pl.BlockSpec((1, width, points), lambda i: (i, 0, 0)),
        compiler_params=params(24),
        cost_estimate=pl.CostEstimate(
            flops=2 * count * width * functions * points,
            bytes_accessed=2 * count * width * points,
            transcendentals=0,
        ),
        name="gather_tables",
    )(index, table)


def collocate(slots, blocks, tables):
    count, both, points = tables.shape
    width = both // 2

    def kernel(slots_ref, blocks_ref, tables_ref, out_ref, held, kept, sems):
        def fetch(j):
            return (
                pltpu.make_async_copy(blocks_ref.at[slots_ref[j]], held.at[j], sems.at[0, j]),
                pltpu.make_async_copy(tables_ref.at[j], kept.at[j], sems.at[1, j]),
            )

        for j in range(count):
            for copy in fetch(j):
                copy.start()
        out_ref[...] = jnp.zeros_like(out_ref)

        def body(j, carry):
            for copy in fetch(j):
                copy.wait()
            product = jnp.dot(held[j], kept[j, width:, :], preferred_element_type=jnp.float32)
            term = kept[j, :width, :].astype(jnp.float32) * product
            out_ref[...] += jnp.sum(term.reshape(width // 8, 8, points), axis=0)
            return carry

        lax.fori_loop(0, count, body, 0)

    return pl.pallas_call(
        kernel,
        out_shape=jax.ShapeDtypeStruct((8, points), jnp.float32),
        in_specs=[SCALARS, IN_HBM, IN_HBM],
        out_specs=RESIDENT,
        scratch_shapes=[
            pltpu.VMEM((count, width, width), jnp.bfloat16),
            pltpu.VMEM(tables.shape, tables.dtype),
            pltpu.SemaphoreType.DMA((2, count)),
        ],
        compiler_params=params(52),
        name="collocate",
    )(slots, blocks, tables)


def integrate(places, scaled, tables, parts, inner):
    count, both, points = tables.shape
    width = both // 2

    def kernel(places_ref, scaled_ref, tables_ref, *rest):
        outs, (held, kept, sems) = rest[:parts], rest[parts:]

        def fetch(j):
            return pltpu.make_async_copy(tables_ref.at[j], kept.at[j], sems.at[0, j])

        def leave(j, part):
            return pltpu.make_async_copy(held.at[j], outs[part].at[places_ref[1, j]], sems.at[1, j])

        for j in range(count):
            fetch(j).start()

        def body(j, carry):
            fetch(j).wait()
            weighted = (kept[j, width:, :].astype(jnp.float32) * scaled_ref[...]).astype(
                jnp.bfloat16
            )
            held[j] = lax.dot_general(
                kept[j, :width, :],
                weighted,
                (((1,), (1,)), ((), ())),
                preferred_element_type=jnp.float32,
            ).astype(jnp.bfloat16)
            for part in range(parts):

                @pl.when(places_ref[0, j] == part)
                def _():
                    leave(j, part).start()

            return carry

        lax.fori_loop(0, count, body, 0)
        for j in range(count):
            leave(j, 0).wait()

    return pl.pallas_call(
        kernel,
        out_shape=[pltpu.HBM((inner, width, width), jnp.bfloat16)] * parts,
        in_specs=[SCALARS, RESIDENT, IN_HBM],
        out_specs=[IN_HBM] * parts,
        scratch_shapes=[
            pltpu.VMEM((count, width, width), jnp.bfloat16),
            pltpu.VMEM(tables.shape, tables.dtype),
            pltpu.SemaphoreType.DMA((2, count)),
        ],
        compiler_params=params(52),
        name="integrate",
    )(places, scaled, tables)


def add_up(targets, parts, place, own_count, dtype):
    _, rows, cols = parts[0].shape
    count = len(parts)

    def kernel(targets_ref, *refs):
        parts_refs, (out_ref, held, total, sems) = refs[:count], refs[count:]

        def fetch(s):
            return pltpu.make_async_copy(parts_refs[s].at[place], held.at[s], sems.at[s])

        for s in range(count):

            @pl.when(targets_ref[s] >= 0)
            def _():
                fetch(s).start()

        total[...] = jnp.zeros_like(total)
        for s in range(count):
            target = targets_ref[s]

            @pl.when(target >= 0)
            def _():
                fetch(s).wait()
                total[target] += held[s].astype(jnp.float32)

        out_ref[...] = total[...].astype(dtype)

    return pl.pallas_call(
        kernel,
        out_shape=jax.ShapeDtypeStruct((own_count, rows, cols), dtype),
        in_specs=[SCALARS] + [IN_HBM] * count,
        out_specs=RESIDENT,
        scratch_shapes=[
            pltpu.VMEM((count, rows, cols), jnp.bfloat16),
            pltpu.VMEM((own_count, rows, cols), jnp.float32),
            pltpu.SemaphoreType.DMA((count,)),
        ],
        compiler_params=params(8),
        name="add_up",
    )(targets, *parts)


def ends(block, dim, width):
    size = block.shape[dim]
    return (
        lax.slice_in_dim(block, 0, width, axis=dim),
        lax.slice_in_dim(block, size - width, size, axis=dim),
    )


def extended_ring(block, axis, dim, width):
    count = lax.axis_size(axis)
    low, high = ends(block, dim, width)
    forward = [(i, (i + 1) % count) for i in range(count)]
    backward = [(target, source) for source, target in forward]
    below = lax.ppermute(high, axis, forward)
    above = lax.ppermute(low, axis, backward)
    return jnp.concatenate([below, block, above], axis=dim)


def extended_pairs(block, axis, dim, width):
    count = size_of(axis)
    odd = lax.axis_index(axis) % 2 == 1
    low, high = ends(block, dim, width)
    within = [(i, i ^ 1) for i in range(count)]
    between = [(i, (i + 1) % count if i % 2 else (i - 1) % count) for i in range(count)]
    far = lax.ppermute(jnp.where(odd, high, low), axis, between)
    near = lax.ppermute(jnp.where(odd, low, high), axis, within)
    below = jnp.where(odd, near, far)
    above = jnp.where(odd, far, near)
    return jnp.concatenate([below, block, above], axis=dim)


def middle(field, dim, width=1):
    return lax.slice_in_dim(field, width, field.shape[dim] - width, axis=dim)


def slope(field, dim):
    size = field.shape[dim]
    return (
        lax.slice_in_dim(field, 2, size, axis=dim) - lax.slice_in_dim(field, 0, size - 2, axis=dim)
    ) * 0.5


def slope_z(field):
    return (jnp.roll(field, -1, 2) - jnp.roll(field, 1, 2)) * 0.5


def potential_of(padded):
    grad_x = middle(slope(padded, 0), 1)
    grad_y = middle(slope(padded, 1), 0)
    centre = middle(middle(padded, 0), 1)
    grad_z = slope_z(centre)
    sigma = grad_x * grad_x + grad_y * grad_y + grad_z * grad_z
    factor = 2.0 * GRAD_WEIGHT / (1.0 + sigma)
    flux_z = middle(middle(factor * grad_z, 0), 1)
    diverge = (
        middle(slope(factor * grad_x, 0), 1) + middle(slope(factor * grad_y, 1), 0) + slope_z(flux_z)
    )
    density = middle(middle(centre, 0), 1)
    return density / jnp.sqrt(1.0 + density * density) - diverge


def size_of(axes):
    return math.prod(lax.axis_size(axis) for axis in axes)


def moved(value, stage, step, other=False):
    nx, ny, nc = (lax.axis_size(axis) for axis in BRICK)
    pairs = []
    for x in range(nx):
        for y in range(ny):
            for c in range(nc):
                core = (c + 1) % nc if other else c
                along_y = (core == 0) == (stage == 1)
                to_x, to_y = (x, (y + step) % ny) if along_y else ((x + step) % nx, y)
                pairs.append(((x * ny + y) * nc + c, (to_x * ny + to_y) * nc + core))
    return lax.ppermute(value, BRICK, pairs)


def find(owners, ids, bricks, wanted):
    hit = owners[bricks][:, None, :] == wanted[None, :, None]
    number = jnp.sum(jnp.where(hit, ids[bricks][:, None, :], 0), axis=-1)
    return jnp.where(jnp.any(hit, axis=-1), number, -1).astype(jnp.int32)


def local(store, crossing, phi, rows_index, cols_index):
    nx, ny, nc = (lax.axis_size(axis) for axis in BRICK)
    x, y, c = (lax.axis_index(axis) for axis in BRICK)
    position = (x * ny + y) * nc + c
    own_count, width = store.shape[0], store.shape[1]
    size_x, size_y, size_z, functions = phi.shape
    points = size_x * size_y * size_z
    owners = crossing // own_count
    ids = crossing % own_count
    chosen = owners == position
    send_ids = jnp.sum(jnp.where(chosen, ids, 0), axis=-1)
    slots = lax.dynamic_index_in_dim(owners, position, 0, keepdims=False)

    sending = pick_blocks(send_ids, store)
    blocks = lax.all_to_all(sending, BRICK, split_axis=0, concat_axis=0, tiled=True)
    table = phi.reshape(points, functions).T
    index = jnp.concatenate([rows_index[0], cols_index[0]], axis=1)[:, None, :]
    tables = gather_tables(index, table)
    density = jnp.sum(collocate(slots, blocks, tables), axis=0).reshape(size_x, size_y, size_z)
    padded = extended_pairs(extended_ring(density, "grp", 0, 2), BRICK, 1, 2)
    scaled = potential_of(padded).reshape(1, points) * (1.0 / math.sqrt(points))

    to_x, rest = slots // (ny * nc), slots % (ny * nc)
    to_y, to_c = rest // nc, rest % nc
    ahead_x, ahead_y = (to_x - x) % nx, (to_y - y) % ny
    side = nx
    first = jnp.where(to_c == 0, ahead_y, ahead_x)
    second = jnp.where(to_c == 0, ahead_x, ahead_y)
    places = jnp.stack([first + jnp.where(to_c == c, 0, side), second]).astype(jnp.int32)
    parts = list(integrate(places, scaled, tables, 2 * side, side))
    for step in [side // 2] + [k for k in range(side) if k not in (side // 2, 0)] + [0]:
        for other in (0, 1):
            if step or other:
                i = other * side + step
                parts[i] = moved(parts[i], 1, step, bool(other))
    steps = jnp.arange(side)
    behind = jnp.where(c == 0, x * ny + (y - steps) % ny, ((x - steps) % nx) * ny + y) * nc
    sources = jnp.concatenate([behind + c, behind + (1 - c)])
    wanted = jnp.where(c == 0, ((x + steps) % nx) * ny + y, x * ny + (y + steps) % ny) * nc + c
    targets = find(owners, ids, sources, wanted)
    total = []
    for step in [side // 2] + [k for k in range(side) if k not in (side // 2, 0)]:
        summed = add_up(targets[:, step], parts, step, own_count, jnp.bfloat16)
        total.append(moved(summed, 2, step))
    own = add_up(targets[:, 0], parts, 0, own_count, jnp.float32)
    for piece in total:
        own = own + piece.astype(jnp.float32)
    return own


def solution(mesh):
    groups, bricks = mesh.shape["grp"], mesh.shape["brick"]
    side = math.isqrt(bricks // 2)
    split = Mesh(mesh.devices.reshape(groups, side, bricks // (2 * side), 2), ("grp",) + BRICK)
    whole = ("grp",) + BRICK
    in_specs = (
        P(whole, None, None),
        P("grp", None),
        P("grp", BRICK, None, None),
        P(whole, None, None),
        P(whole, None, None),
    )
    return jax.shard_map(
        local, mesh=split, in_specs=in_specs, out_specs=P(whole, None, None), check_vma=False
    )
```

```python
import math

import jax
import jax.numpy as jnp
from jax import lax
from jax.experimental import pallas as pl
from jax.experimental.pallas import tpu as pltpu
from jax.sharding import Mesh
from jax.sharding import PartitionSpec as P

GRAD_WEIGHT = 0.5
GATHERS = 4
BRICK = ("x", "y", "core")
MIB = 1024 * 1024


RESIDENT = pl.BlockSpec(memory_space=pltpu.VMEM)
IN_HBM = pl.BlockSpec(memory_space=pltpu.HBM)
SCALARS = pl.BlockSpec(memory_space=pltpu.SMEM)


def params(mib):
    return pltpu.CompilerParams(vmem_limit_bytes=mib * MIB)


def select_blocks(numbers, stores, parts):
    inner = len(stores)
    block = stores[0].shape[1:]

    def kernel(numbers_ref, *refs):
        ins, outs, sems = refs[:inner], refs[inner:-1], refs[-1]
        places = [(p, d) for p in range(parts) for d in range(inner)]

        def copy(p, d):
            number = jnp.maximum(numbers_ref[p, d], 0)
            return pltpu.make_async_copy(ins[d].at[number], outs[p].at[d], sems.at[p, d])

        for p, d in places:

            @pl.when(numbers_ref[p, d] >= 0)
            def _():
                copy(p, d).start()

        for p, d in places:

            @pl.when(numbers_ref[p, d] >= 0)
            def _():
                copy(p, d).wait()

    return pl.pallas_call(
        kernel,
        out_shape=[pltpu.HBM((inner,) + block, stores[0].dtype)] * parts,
        in_specs=[SCALARS] + [IN_HBM] * inner,
        out_specs=[IN_HBM] * parts,
        scratch_shapes=[pltpu.SemaphoreType.DMA((parts, inner))],
        compiler_params=params(4),
        name="select_blocks",
    )(numbers, *stores)


def gather_tables(index, table):
    count, _, width = index.shape
    functions, points = table.shape
    lanes = 128

    def kernel(index_ref, table_ref, out_ref):
        pieces = []
        for start in range(0, width, lanes):
            row = index_ref[0, :, start : start + lanes]
            column = jnp.broadcast_to(row, (lanes, lanes)).T
            hot = [
                jnp.where(
                    column == lax.broadcasted_iota(jnp.int32, (lanes, lanes), 1) + f, 1.0, 0.0
                ).astype(jnp.bfloat16)
                for f in range(0, functions, lanes)
            ]
            pieces.append(jnp.concatenate(hot, axis=1))
        onehot = jnp.concatenate(pieces, axis=0)
        out_ref[0] = jnp.dot(
            onehot, table_ref[...], preferred_element_type=jnp.float32
        ).astype(jnp.bfloat16)

    return pl.pallas_call(
        kernel,
        out_shape=pltpu.HBM((count, width, points), jnp.bfloat16),
        grid=(count,),
        in_specs=[
            pl.BlockSpec((1, 1, width), lambda i: (i, 0, 0)),
            pl.BlockSpec((functions, points), lambda i: (0, 0)),
        ],
        out_specs=pl.BlockSpec((1, width, points), lambda i: (i, 0, 0)),
        compiler_params=params(24),
        cost_estimate=pl.CostEstimate(
            flops=2 * count * width * functions * points,
            bytes_accessed=2 * count * width * points,
            transcendentals=0,
        ),
        name="gather_tables",
    )(index, table)


def collocate(places, blocks, tables):
    each, both, points = tables[0].shape
    count = each * len(tables)
    width = both // 2
    parts = len(blocks)

    def kernel(places_ref, *refs):
        blocks_refs, tables_refs = refs[:parts], refs[parts:-4]
        out_ref, held, kept, sems = refs[-4:]

        def fetch_block(j, part):
            return pltpu.make_async_copy(
                blocks_refs[part].at[places_ref[1, j]], held.at[j], sems.at[0, j]
            )

        def fetch_table(j, ref, place):
            return pltpu.make_async_copy(ref.at[place], kept.at[j], sems.at[1, j])

        for j in range(count):
            for part in range(parts):

                @pl.when(places_ref[0, j] == part)
                def _():
                    fetch_block(j, part).start()

            fetch_table(j, tables_refs[j // each], j % each).start()
        out_ref[...] = jnp.zeros_like(out_ref)

        def body(j, carry):
            fetch_block(j, 0).wait()
            fetch_table(j, tables_refs[0], 0).wait()
            product = jnp.dot(held[j], kept[j, width:, :], preferred_element_type=jnp.float32)
            term = kept[j, :width, :].astype(jnp.float32) * product
            out_ref[...] += jnp.sum(term.reshape(width // 8, 8, points), axis=0)
            return carry

        lax.fori_loop(0, count, body, 0)

    return pl.pallas_call(
        kernel,
        out_shape=jax.ShapeDtypeStruct((8, points), jnp.float32),
        in_specs=[SCALARS] + [IN_HBM] * (parts + len(tables)),
        out_specs=RESIDENT,
        scratch_shapes=[
            pltpu.VMEM((count, width, width), jnp.bfloat16),
            pltpu.VMEM((count, both, points), jnp.bfloat16),
            pltpu.SemaphoreType.DMA((2, count)),
        ],
        compiler_params=params(52),
        name="collocate",
    )(places, *blocks, *tables)


def integrate(places, scaled, tables, parts, inner):
    each, both, points = tables[0].shape
    count = each * len(tables)
    width = both // 2

    def kernel(places_ref, scaled_ref, *refs):
        tables_refs, outs = refs[: len(tables)], refs[len(tables) : -3]
        held, kept, sems = refs[-3:]

        def fetch(j, ref, place):
            return pltpu.make_async_copy(ref.at[place], kept.at[j], sems.at[0, j])

        def leave(j, part):
            return pltpu.make_async_copy(held.at[j], outs[part].at[places_ref[1, j]], sems.at[1, j])

        for j in range(count):
            fetch(j, tables_refs[j // each], j % each).start()

        def body(j, carry):
            fetch(j, tables_refs[0], 0).wait()
            weighted = (kept[j, width:, :].astype(jnp.float32) * scaled_ref[...]).astype(
                jnp.bfloat16
            )
            held[j] = lax.dot_general(
                kept[j, :width, :],
                weighted,
                (((1,), (1,)), ((), ())),
                preferred_element_type=jnp.float32,
            ).astype(jnp.bfloat16)
            for part in range(parts):

                @pl.when(places_ref[0, j] == part)
                def _():
                    leave(j, part).start()

            return carry

        lax.fori_loop(0, count, body, 0)
        for j in range(count):
            leave(j, 0).wait()

    return pl.pallas_call(
        kernel,
        out_shape=[pltpu.HBM((inner, width, width), jnp.bfloat16)] * parts,
        in_specs=[SCALARS, RESIDENT] + [IN_HBM] * len(tables),
        out_specs=[IN_HBM] * parts,
        scratch_shapes=[
            pltpu.VMEM((count, width, width), jnp.bfloat16),
            pltpu.VMEM((count, both, points), jnp.bfloat16),
            pltpu.SemaphoreType.DMA((2, count)),
        ],
        compiler_params=params(52),
        name="integrate",
    )(places, scaled, *tables)


def add_up(targets, parts, place, own_count, dtype):
    _, rows, cols = parts[0].shape
    count = len(parts)

    def kernel(targets_ref, *refs):
        parts_refs, (out_ref, held, total, sems) = refs[:count], refs[count:]

        def fetch(s):
            return pltpu.make_async_copy(parts_refs[s].at[place], held.at[s], sems.at[s])

        for s in range(count):

            @pl.when(targets_ref[s] >= 0)
            def _():
                fetch(s).start()

        total[...] = jnp.zeros_like(total)
        for s in range(count):
            target = targets_ref[s]

            @pl.when(target >= 0)
            def _():
                fetch(s).wait()
                total[target] += held[s].astype(jnp.float32)

        out_ref[...] = total[...].astype(dtype)

    return pl.pallas_call(
        kernel,
        out_shape=jax.ShapeDtypeStruct((own_count, rows, cols), dtype),
        in_specs=[SCALARS] + [IN_HBM] * count,
        out_specs=RESIDENT,
        scratch_shapes=[
            pltpu.VMEM((count, rows, cols), jnp.bfloat16),
            pltpu.VMEM((own_count, rows, cols), jnp.float32),
            pltpu.SemaphoreType.DMA((count,)),
        ],
        compiler_params=params(8),
        name="add_up",
    )(targets, *parts)


def ends(block, dim, width):
    size = block.shape[dim]
    return (
        lax.slice_in_dim(block, 0, width, axis=dim),
        lax.slice_in_dim(block, size - width, size, axis=dim),
    )


def extended_ring(block, axis, dim, width):
    count = lax.axis_size(axis)
    low, high = ends(block, dim, width)
    forward = [(i, (i + 1) % count) for i in range(count)]
    backward = [(target, source) for source, target in forward]
    below = lax.ppermute(high, axis, forward)
    above = lax.ppermute(low, axis, backward)
    return jnp.concatenate([below, block, above], axis=dim)


def extended_pairs(block, axis, dim, width):
    count = size_of(axis)
    odd = lax.axis_index(axis) % 2 == 1
    low, high = ends(block, dim, width)
    within = [(i, i ^ 1) for i in range(count)]
    between = [(i, (i + 1) % count if i % 2 else (i - 1) % count) for i in range(count)]
    far = lax.ppermute(jnp.where(odd, high, low), axis, between)
    near = lax.ppermute(jnp.where(odd, low, high), axis, within)
    below = jnp.where(odd, near, far)
    above = jnp.where(odd, far, near)
    return jnp.concatenate([below, block, above], axis=dim)


def middle(field, dim, width=1):
    return lax.slice_in_dim(field, width, field.shape[dim] - width, axis=dim)


def slope(field, dim):
    size = field.shape[dim]
    return (
        lax.slice_in_dim(field, 2, size, axis=dim) - lax.slice_in_dim(field, 0, size - 2, axis=dim)
    ) * 0.5


def slope_z(field):
    return (jnp.roll(field, -1, 2) - jnp.roll(field, 1, 2)) * 0.5


def potential_of(padded):
    grad_x = middle(slope(padded, 0), 1)
    grad_y = middle(slope(padded, 1), 0)
    centre = middle(middle(padded, 0), 1)
    grad_z = slope_z(centre)
    sigma = grad_x * grad_x + grad_y * grad_y + grad_z * grad_z
    factor = 2.0 * GRAD_WEIGHT / (1.0 + sigma)
    flux_z = middle(middle(factor * grad_z, 0), 1)
    diverge = (
        middle(slope(factor * grad_x, 0), 1) + middle(slope(factor * grad_y, 1), 0) + slope_z(flux_z)
    )
    density = middle(middle(centre, 0), 1)
    return density / jnp.sqrt(1.0 + density * density) - diverge


def size_of(axes):
    return math.prod(lax.axis_size(axis) for axis in axes)


def moved(value, step, other, along):
    nx, ny, nc = (lax.axis_size(axis) for axis in BRICK)
    pairs = []
    for x in range(nx):
        for y in range(ny):
            for c in range(nc):
                core = (c + 1) % nc if other else c
                to_x, to_y = (x, (y + step) % ny) if along(c, core) else ((x + step) % nx, y)
                pairs.append(((x * ny + y) * nc + c, (to_x * ny + to_y) * nc + core))
    return lax.ppermute(value, BRICK, pairs)


def order(side):
    return [side // 2] + [k for k in range(side) if k not in (side // 2, 0)]


def find(owners, ids, bricks, wanted):
    hit = owners[bricks][:, None, :] == wanted[None, :, None]
    number = jnp.sum(jnp.where(hit, ids[bricks][:, None, :], 0), axis=-1)
    return jnp.where(jnp.any(hit, axis=-1), number, -1).astype(jnp.int32)


def local(store, crossing, phi, rows_index, cols_index):
    nx, ny, nc = (lax.axis_size(axis) for axis in BRICK)
    x, y, c = (lax.axis_index(axis) for axis in BRICK)
    position = (x * ny + y) * nc + c
    own_count, width = store.shape[0], store.shape[1]
    size_x, size_y, size_z, functions = phi.shape
    points = size_x * size_y * size_z
    owners = crossing // own_count
    ids = crossing % own_count
    slots = lax.dynamic_index_in_dim(owners, position, 0, keepdims=False)
    side = nx
    steps = jnp.arange(side)

    stores = [store] + [None] * (side - 1)
    for step in order(side):
        stores[step] = moved(store, step, False, lambda c, to: c == 1)
    table = phi.reshape(points, functions).T
    index = jnp.concatenate([rows_index[0], cols_index[0]], axis=1)[:, None, :]
    each = index.shape[0] // GATHERS
    tables = [gather_tables(index[i : i + each], table) for i in range(0, index.shape[0], each)]
    ahead = jnp.where(c == 0, x * ny + (y + steps) % ny, ((x + steps) % nx) * ny + y) * nc
    served = jnp.concatenate([ahead + c, ahead + (1 - c)])
    source = jnp.where(c == 0, ((x - steps) % nx) * ny + y, x * ny + (y - steps) % ny) * nc + c
    blocks = list(select_blocks(find(owners, ids, served, source), stores, 2 * side))
    for step in order(side) + [0]:
        for other in (0, 1):
            if step or other:
                i = other * side + step
                blocks[i] = moved(blocks[i], step, bool(other), lambda c, to: c == 0)
    to_x, rest = slots // (ny * nc), slots % (ny * nc)
    to_y, to_c = rest // nc, rest % nc
    behind_x, behind_y = (x - to_x) % nx, (y - to_y) % ny
    last = jnp.where(to_c == 0, behind_y, behind_x) + jnp.where(to_c == c, 0, side)
    places = jnp.stack([last, jnp.where(to_c == 0, behind_x, behind_y)]).astype(jnp.int32)
    layers = collocate(places, blocks, tables)
    density = jnp.sum(layers, axis=0).reshape(size_x, size_y, size_z)
    padded = extended_pairs(extended_ring(density, "grp", 0, 2), BRICK, 1, 2)
    scaled = potential_of(padded).reshape(1, points) * (1.0 / math.sqrt(points))

    ahead_x, ahead_y = (to_x - x) % nx, (to_y - y) % ny
    first = jnp.where(to_c == 0, ahead_y, ahead_x)
    second = jnp.where(to_c == 0, ahead_x, ahead_y)
    places = jnp.stack([first + jnp.where(to_c == c, 0, side), second]).astype(jnp.int32)
    parts = list(integrate(places, scaled, tables, 2 * side, side))
    for step in order(side) + [0]:
        for other in (0, 1):
            if step or other:
                i = other * side + step
                parts[i] = moved(parts[i], step, bool(other), lambda c, to: to == 0)
    behind = jnp.where(c == 0, x * ny + (y - steps) % ny, ((x - steps) % nx) * ny + y) * nc
    sources = jnp.concatenate([behind + c, behind + (1 - c)])
    wanted = jnp.where(c == 0, ((x + steps) % nx) * ny + y, x * ny + (y + steps) % ny) * nc + c
    targets = find(owners, ids, sources, wanted)
    total = []
    for step in order(side):
        summed = add_up(targets[:, step], parts, step, own_count, jnp.bfloat16)
        total.append(moved(summed, step, False, lambda c, to: c == 1))
    own = add_up(targets[:, 0], parts, 0, own_count, jnp.float32)
    for piece in total:
        own = own + piece.astype(jnp.float32)
    return own


def solution(mesh):
    groups, bricks = mesh.shape["grp"], mesh.shape["brick"]
    side = math.isqrt(bricks // 2)
    split = Mesh(mesh.devices.reshape(groups, side, bricks // (2 * side), 2), ("grp",) + BRICK)
    whole = ("grp",) + BRICK
    in_specs = (
        P(whole, None, None),
        P("grp", None),
        P("grp", BRICK, None, None),
        P(whole, None, None),
        P(whole, None, None),
    )
    return jax.shard_map(
        local, mesh=split, in_specs=in_specs, out_specs=P(whole, None, None), check_vma=False
    )
```

```python
import math

import jax
import jax.numpy as jnp
from jax import lax
from jax.experimental import pallas as pl
from jax.experimental.pallas import tpu as pltpu
from jax.sharding import Mesh
from jax.sharding import PartitionSpec as P

GRAD_WEIGHT = 0.5
GATHERS = 4
BRICK = ("x", "y", "core")
MIB = 1024 * 1024


RESIDENT = pl.BlockSpec(memory_space=pltpu.VMEM)
IN_HBM = pl.BlockSpec(memory_space=pltpu.HBM)
SCALARS = pl.BlockSpec(memory_space=pltpu.SMEM)


def params(mib):
    return pltpu.CompilerParams(vmem_limit_bytes=mib * MIB)


def select_blocks(bricks, numbers, stores):
    inner, parts = len(stores), bricks.shape[0]
    block = stores[0].shape[1:]

    def kernel(bricks_ref, numbers_ref, *refs):
        ins, outs, sems = refs[:inner], refs[inner:-1], refs[-1]
        places = [(p, d) for p in range(parts) for d in range(inner)]

        def copy(p, d):
            number = jnp.maximum(numbers_ref[bricks_ref[p], d], 0)
            return pltpu.make_async_copy(ins[d].at[number], outs[p].at[d], sems.at[p, d])

        for p, d in places:

            @pl.when(numbers_ref[bricks_ref[p], d] >= 0)
            def _():
                copy(p, d).start()

        for p, d in places:

            @pl.when(numbers_ref[bricks_ref[p], d] >= 0)
            def _():
                copy(p, d).wait()

    return pl.pallas_call(
        kernel,
        out_shape=[pltpu.HBM((inner,) + block, stores[0].dtype)] * parts,
        in_specs=[SCALARS, SCALARS] + [IN_HBM] * inner,
        out_specs=[IN_HBM] * parts,
        scratch_shapes=[pltpu.SemaphoreType.DMA((parts, inner))],
        compiler_params=params(4),
        name="select_blocks",
    )(bricks, numbers, *stores)


def gather_tables(index, table):
    count, _, width = index.shape
    functions, points = table.shape
    lanes = 128

    def kernel(index_ref, table_ref, out_ref):
        pieces = []
        for start in range(0, width, lanes):
            row = index_ref[0, :, start : start + lanes]
            column = jnp.broadcast_to(row, (lanes, lanes)).T
            hot = [
                jnp.where(
                    column == lax.broadcasted_iota(jnp.int32, (lanes, lanes), 1) + f, 1.0, 0.0
                ).astype(jnp.bfloat16)
                for f in range(0, functions, lanes)
            ]
            pieces.append(jnp.concatenate(hot, axis=1))
        onehot = jnp.concatenate(pieces, axis=0)
        out_ref[0] = jnp.dot(
            onehot, table_ref[...], preferred_element_type=jnp.float32
        ).astype(jnp.bfloat16)

    return pl.pallas_call(
        kernel,
        out_shape=pltpu.HBM((count, width, points), jnp.bfloat16),
        grid=(count,),
        in_specs=[
            pl.BlockSpec((1, 1, width), lambda i: (i, 0, 0)),
            pl.BlockSpec((functions, points), lambda i: (0, 0)),
        ],
        out_specs=pl.BlockSpec((1, width, points), lambda i: (i, 0, 0)),
        compiler_params=params(24),
        cost_estimate=pl.CostEstimate(
            flops=2 * count * width * functions * points,
            bytes_accessed=2 * count * width * points,
            transcendentals=0,
        ),
        name="gather_tables",
    )(index, table)


def collocate(places, blocks, tables):
    each, both, points = tables[0].shape
    count = each * len(tables)
    width = both // 2
    parts = len(blocks)

    def kernel(places_ref, *refs):
        blocks_refs, tables_refs = refs[:parts], refs[parts:-4]
        out_ref, held, kept, sems = refs[-4:]

        def fetch_block(j, part):
            return pltpu.make_async_copy(
                blocks_refs[part].at[places_ref[1, j]], held.at[j], sems.at[0, j]
            )

        def fetch_table(j, ref, place):
            return pltpu.make_async_copy(ref.at[place], kept.at[j], sems.at[1, j])

        for j in range(count):
            for part in range(parts):

                @pl.when(places_ref[0, j] == part)
                def _():
                    fetch_block(j, part).start()

            fetch_table(j, tables_refs[j // each], j % each).start()
        out_ref[...] = jnp.zeros_like(out_ref)

        def body(j, carry):
            fetch_block(j, 0).wait()
            fetch_table(j, tables_refs[0], 0).wait()
            product = jnp.dot(held[j], kept[j, width:, :], preferred_element_type=jnp.float32)
            term = kept[j, :width, :].astype(jnp.float32) * product
            out_ref[...] += jnp.sum(term.reshape(width // 8, 8, points), axis=0)
            return carry

        lax.fori_loop(0, count, body, 0)

    return pl.pallas_call(
        kernel,
        out_shape=jax.ShapeDtypeStruct((8, points), jnp.float32),
        in_specs=[SCALARS] + [IN_HBM] * (parts + len(tables)),
        out_specs=RESIDENT,
        scratch_shapes=[
            pltpu.VMEM((count, width, width), jnp.bfloat16),
            pltpu.VMEM((count, both, points), jnp.bfloat16),
            pltpu.SemaphoreType.DMA((2, count)),
        ],
        compiler_params=params(48),
        name="collocate",
    )(places, *blocks, *tables)


def integrate(places, scaled, tables, parts, inner):
    each, both, points = tables[0].shape
    count = each * len(tables)
    width = both // 2

    def kernel(places_ref, scaled_ref, *refs):
        tables_refs, outs = refs[: len(tables)], refs[len(tables) : -3]
        held, kept, sems = refs[-3:]

        def fetch(j, ref, place):
            return pltpu.make_async_copy(ref.at[place], kept.at[j], sems.at[0, j])

        def leave(j, part):
            return pltpu.make_async_copy(held.at[j], outs[part].at[places_ref[1, j]], sems.at[1, j])

        for j in range(count):
            fetch(j, tables_refs[j // each], j % each).start()

        def body(j, carry):
            fetch(j, tables_refs[0], 0).wait()
            weighted = (kept[j, width:, :].astype(jnp.float32) * scaled_ref[...]).astype(
                jnp.bfloat16
            )
            held[j] = lax.dot_general(
                kept[j, :width, :],
                weighted,
                (((1,), (1,)), ((), ())),
                preferred_element_type=jnp.float32,
            ).astype(jnp.bfloat16)
            for part in range(parts):

                @pl.when(places_ref[0, j] == part)
                def _():
                    leave(j, part).start()

            return carry

        lax.fori_loop(0, count, body, 0)
        for j in range(count):
            leave(j, 0).wait()

    return pl.pallas_call(
        kernel,
        out_shape=[pltpu.HBM((inner, width, width), jnp.bfloat16)] * parts,
        in_specs=[SCALARS, RESIDENT] + [IN_HBM] * len(tables),
        out_specs=[IN_HBM] * parts,
        scratch_shapes=[
            pltpu.VMEM((count, width, width), jnp.bfloat16),
            pltpu.VMEM((count, both, points), jnp.bfloat16),
            pltpu.SemaphoreType.DMA((2, count)),
        ],
        compiler_params=params(52),
        name="integrate",
    )(places, scaled, *tables)


def add_up(bricks, numbers, parts, place, own_count, dtype):
    _, rows, cols = parts[0].shape
    count = len(parts)

    def kernel(bricks_ref, numbers_ref, *refs):
        parts_refs, (out_ref, held, total, sems) = refs[:count], refs[count:]

        def fetch(s):
            return pltpu.make_async_copy(parts_refs[s].at[place], held.at[s], sems.at[s])

        for s in range(count):

            @pl.when(numbers_ref[bricks_ref[s], place] >= 0)
            def _():
                fetch(s).start()

        total[...] = jnp.zeros_like(total)
        for s in range(count):
            target = numbers_ref[bricks_ref[s], place]

            @pl.when(target >= 0)
            def _():
                fetch(s).wait()
                total[target] += held[s].astype(jnp.float32)

        out_ref[...] = total[...].astype(dtype)

    return pl.pallas_call(
        kernel,
        out_shape=jax.ShapeDtypeStruct((own_count, rows, cols), dtype),
        in_specs=[SCALARS, SCALARS] + [IN_HBM] * count,
        out_specs=RESIDENT,
        scratch_shapes=[
            pltpu.VMEM((count, rows, cols), jnp.bfloat16),
            pltpu.VMEM((own_count, rows, cols), jnp.float32),
            pltpu.SemaphoreType.DMA((count,)),
        ],
        compiler_params=params(8),
        name="add_up",
    )(bricks, numbers, *parts)


def ends(block, dim, width):
    size = block.shape[dim]
    return (
        lax.slice_in_dim(block, 0, width, axis=dim),
        lax.slice_in_dim(block, size - width, size, axis=dim),
    )


def extended_ring(block, axis, dim, width):
    count = lax.axis_size(axis)
    low, high = ends(block, dim, width)
    forward = [(i, (i + 1) % count) for i in range(count)]
    backward = [(target, source) for source, target in forward]
    below = lax.ppermute(high, axis, forward)
    above = lax.ppermute(low, axis, backward)
    return jnp.concatenate([below, block, above], axis=dim)


def extended_pairs(block, axis, dim, width):
    count = size_of(axis)
    odd = lax.axis_index(axis) % 2 == 1
    low, high = ends(block, dim, width)
    within = [(i, i ^ 1) for i in range(count)]
    between = [(i, (i + 1) % count if i % 2 else (i - 1) % count) for i in range(count)]
    far = lax.ppermute(jnp.where(odd, high, low), axis, between)
    near = lax.ppermute(jnp.where(odd, low, high), axis, within)
    below = jnp.where(odd, near, far)
    above = jnp.where(odd, far, near)
    return jnp.concatenate([below, block, above], axis=dim)


def middle(field, dim, width=1):
    return lax.slice_in_dim(field, width, field.shape[dim] - width, axis=dim)


def slope(field, dim):
    size = field.shape[dim]
    return (
        lax.slice_in_dim(field, 2, size, axis=dim) - lax.slice_in_dim(field, 0, size - 2, axis=dim)
    ) * 0.5


def slope_z(field):
    return (jnp.roll(field, -1, 2) - jnp.roll(field, 1, 2)) * 0.5


def potential_of(padded):
    grad_x = middle(slope(padded, 0), 1)
    grad_y = middle(slope(padded, 1), 0)
    centre = middle(middle(padded, 0), 1)
    grad_z = slope_z(centre)
    sigma = grad_x * grad_x + grad_y * grad_y + grad_z * grad_z
    factor = 2.0 * GRAD_WEIGHT / (1.0 + sigma)
    flux_z = middle(middle(factor * grad_z, 0), 1)
    diverge = (
        middle(slope(factor * grad_x, 0), 1) + middle(slope(factor * grad_y, 1), 0) + slope_z(flux_z)
    )
    density = middle(middle(centre, 0), 1)
    return density / jnp.sqrt(1.0 + density * density) - diverge


def size_of(axes):
    return math.prod(lax.axis_size(axis) for axis in axes)


def moved(value, step, other, along):
    nx, ny, nc = (lax.axis_size(axis) for axis in BRICK)
    pairs = []
    for x in range(nx):
        for y in range(ny):
            for c in range(nc):
                core = (c + 1) % nc if other else c
                to_x, to_y = (x, (y + step) % ny) if along(c, core) else ((x + step) % nx, y)
                pairs.append(((x * ny + y) * nc + c, (to_x * ny + to_y) * nc + core))
    return lax.ppermute(value, BRICK, pairs)


def turns(side):
    near = [1, side - 1]
    far = [k for k in range(side) if k not in (0, 1, side - 1)]
    return [(o, k) for o in (0, 1) for k in near] + [(o, k) for k in far for o in (0, 1)] + [(1, 0)]


def order(side):
    return [side // 2] + [k for k in range(side) if k not in (side // 2, 0)]


def find(owners, ids, wanted):
    hit = owners[:, None, :] == wanted[None, :, None]
    return jnp.max(jnp.where(hit, ids[:, None, :], -1), axis=-1).astype(jnp.int32)


def local(store, crossing, phi, rows_index, cols_index):
    nx, ny, nc = (lax.axis_size(axis) for axis in BRICK)
    x, y, c = (lax.axis_index(axis) for axis in BRICK)
    position = (x * ny + y) * nc + c
    own_count, width = store.shape[0], store.shape[1]
    size_x, size_y, size_z, functions = phi.shape
    points = size_x * size_y * size_z
    owners = crossing // own_count
    ids = crossing % own_count
    slots = lax.dynamic_index_in_dim(owners, position, 0, keepdims=False)
    side = nx
    steps = jnp.arange(side)

    stores = [store] + [None] * (side - 1)
    for step in order(side):
        stores[step] = moved(store, step, False, lambda c, to: c == 1)
    table = phi.reshape(points, functions).T
    index = jnp.concatenate([rows_index[0], cols_index[0]], axis=1)[:, None, :]
    each = index.shape[0] // GATHERS
    pieces = [index[i : i + each] for i in range(0, index.shape[0], each)]
    ahead = jnp.where(c == 0, x * ny + (y + steps) % ny, ((x + steps) % nx) * ny + y) * nc
    served = jnp.concatenate([ahead + c, ahead + (1 - c)]).astype(jnp.int32)
    source = jnp.where(c == 0, ((x - steps) % nx) * ny + y, x * ny + (y - steps) % ny) * nc + c
    blocks = list(select_blocks(served, find(owners, ids, source), stores))
    *pieces[1:], blocks[side] = lax.optimization_barrier((*pieces[1:], blocks[side]))
    tables = [gather_tables(piece, table) for piece in pieces]
    for other, step in turns(side):
        i = other * side + step
        blocks[i] = moved(blocks[i], step, bool(other), lambda c, to: c == 0)
    to_x, rest = slots // (ny * nc), slots % (ny * nc)
    to_y, to_c = rest // nc, rest % nc
    behind_x, behind_y = (x - to_x) % nx, (y - to_y) % ny
    last = jnp.where(to_c == 0, behind_y, behind_x) + jnp.where(to_c == c, 0, side)
    places = jnp.stack([last, jnp.where(to_c == 0, behind_x, behind_y)]).astype(jnp.int32)
    layers = collocate(places, blocks, tables)
    density = jnp.sum(layers, axis=0).reshape(size_x, size_y, size_z)
    padded = extended_pairs(extended_ring(density, "grp", 0, 2), BRICK, 1, 2)
    scaled = potential_of(padded).reshape(1, points) * (1.0 / math.sqrt(points))

    ahead_x, ahead_y = (to_x - x) % nx, (to_y - y) % ny
    first = jnp.where(to_c == 0, ahead_y, ahead_x)
    second = jnp.where(to_c == 0, ahead_x, ahead_y)
    places = jnp.stack([first + jnp.where(to_c == c, 0, side), second]).astype(jnp.int32)
    parts = list(integrate(places, scaled, tables, 2 * side, side))
    for other, step in turns(side):
        i = other * side + step
        parts[i] = moved(parts[i], step, bool(other), lambda c, to: to == 0)
    behind = jnp.where(c == 0, x * ny + (y - steps) % ny, ((x - steps) % nx) * ny + y) * nc
    sources = jnp.concatenate([behind + c, behind + (1 - c)]).astype(jnp.int32)
    wanted = jnp.where(c == 0, ((x + steps) % nx) * ny + y, x * ny + (y + steps) % ny) * nc + c
    numbers = find(owners, ids, wanted)
    total = []
    for step in order(side):
        summed = add_up(sources, numbers, parts, step, own_count, jnp.bfloat16)
        total.append(moved(summed, step, False, lambda c, to: c == 1))
    own = add_up(sources, numbers, parts, 0, own_count, jnp.float32)
    for piece in total:
        own = own + piece.astype(jnp.float32)
    return own


def solution(mesh):
    groups, bricks = mesh.shape["grp"], mesh.shape["brick"]
    side = math.isqrt(bricks // 2)
    split = Mesh(mesh.devices.reshape(groups, side, bricks // (2 * side), 2), ("grp",) + BRICK)
    whole = ("grp",) + BRICK
    in_specs = (
        P(whole, None, None),
        P("grp", None),
        P("grp", BRICK, None, None),
        P(whole, None, None),
        P(whole, None, None),
    )
    return jax.shard_map(
        local, mesh=split, in_specs=in_specs, out_specs=P(whole, None, None), check_vma=False
    )
```

```python
import math

import jax
import jax.numpy as jnp
from jax import lax
from jax.experimental import pallas as pl
from jax.experimental.pallas import tpu as pltpu
from jax.sharding import Mesh
from jax.sharding import PartitionSpec as P

GRAD_WEIGHT = 0.5
GATHERS = 4
BRICK = ("x", "y", "core")
MIB = 1024 * 1024


RESIDENT = pl.BlockSpec(memory_space=pltpu.VMEM)
IN_HBM = pl.BlockSpec(memory_space=pltpu.HBM)
SCALARS = pl.BlockSpec(memory_space=pltpu.SMEM)


def params(mib):
    return pltpu.CompilerParams(vmem_limit_bytes=mib * MIB)


def select_blocks(bricks, numbers, stores):
    inner, parts = len(stores), bricks.shape[0]
    block = stores[0].shape[1:]

    def kernel(bricks_ref, numbers_ref, *refs):
        ins, outs, sems = refs[:inner], refs[inner:-1], refs[-1]
        places = [(p, d) for p in range(parts) for d in range(inner)]

        def copy(p, d):
            number = jnp.maximum(numbers_ref[bricks_ref[p], d], 0)
            return pltpu.make_async_copy(ins[d].at[number], outs[p].at[d], sems.at[p, d])

        for p, d in places:

            @pl.when(numbers_ref[bricks_ref[p], d] >= 0)
            def _():
                copy(p, d).start()

        for p, d in places:

            @pl.when(numbers_ref[bricks_ref[p], d] >= 0)
            def _():
                copy(p, d).wait()

    return pl.pallas_call(
        kernel,
        out_shape=[pltpu.HBM((inner,) + block, stores[0].dtype)] * parts,
        in_specs=[SCALARS, SCALARS] + [IN_HBM] * inner,
        out_specs=[IN_HBM] * parts,
        scratch_shapes=[pltpu.SemaphoreType.DMA((parts, inner))],
        compiler_params=params(4),
        name="select_blocks",
    )(bricks, numbers, *stores)


def gather_tables(index, table):
    count, _, width = index.shape
    functions, points = table.shape
    lanes = 128

    def kernel(index_ref, table_ref, out_ref):
        pieces = []
        for start in range(0, width, lanes):
            row = index_ref[0, :, start : start + lanes]
            column = jnp.broadcast_to(row, (lanes, lanes)).T
            hot = [
                jnp.where(
                    column == lax.broadcasted_iota(jnp.int32, (lanes, lanes), 1) + f, 1.0, 0.0
                ).astype(jnp.bfloat16)
                for f in range(0, functions, lanes)
            ]
            pieces.append(jnp.concatenate(hot, axis=1))
        onehot = jnp.concatenate(pieces, axis=0)
        out_ref[0] = jnp.dot(
            onehot, table_ref[...], preferred_element_type=jnp.float32
        ).astype(jnp.bfloat16)

    return pl.pallas_call(
        kernel,
        out_shape=pltpu.HBM((count, width, points), jnp.bfloat16),
        grid=(count,),
        in_specs=[
            pl.BlockSpec((1, 1, width), lambda i: (i, 0, 0)),
            pl.BlockSpec((functions, points), lambda i: (0, 0)),
        ],
        out_specs=pl.BlockSpec((1, width, points), lambda i: (i, 0, 0)),
        compiler_params=params(24),
        cost_estimate=pl.CostEstimate(
            flops=2 * count * width * functions * points,
            bytes_accessed=2 * count * width * points,
            transcendentals=0,
        ),
        name="gather_tables",
    )(index, table)


def collocate(places, blocks, tables):
    each, both, points = tables[0].shape
    count = each * len(tables)
    width = both // 2
    parts = len(blocks)

    def kernel(places_ref, *refs):
        blocks_refs, tables_refs = refs[:parts], refs[parts:-4]
        out_ref, held, kept, sems = refs[-4:]

        def fetch_block(j, part):
            return pltpu.make_async_copy(
                blocks_refs[part].at[places_ref[1, j]], held.at[j], sems.at[0, j]
            )

        def fetch_table(j, ref, place):
            return pltpu.make_async_copy(ref.at[place], kept.at[j], sems.at[1, j])

        for j in range(count):
            for part in range(parts):

                @pl.when(places_ref[0, j] == part)
                def _():
                    fetch_block(j, part).start()

            fetch_table(j, tables_refs[j // each], j % each).start()
        out_ref[...] = jnp.zeros_like(out_ref)

        def body(j, carry):
            fetch_block(j, 0).wait()
            fetch_table(j, tables_refs[0], 0).wait()
            product = jnp.dot(held[j], kept[j, width:, :], preferred_element_type=jnp.float32)
            term = kept[j, :width, :].astype(jnp.float32) * product
            out_ref[...] += jnp.sum(term.reshape(width // 8, 8, points), axis=0)
            return carry

        lax.fori_loop(0, count, body, 0)

    return pl.pallas_call(
        kernel,
        out_shape=jax.ShapeDtypeStruct((8, points), jnp.float32),
        in_specs=[SCALARS] + [IN_HBM] * (parts + len(tables)),
        out_specs=RESIDENT,
        scratch_shapes=[
            pltpu.VMEM((count, width, width), jnp.bfloat16),
            pltpu.VMEM((count, both, points), jnp.bfloat16),
            pltpu.SemaphoreType.DMA((2, count)),
        ],
        compiler_params=params(52),
        name="collocate",
    )(places, *blocks, *tables)


def integrate(places, scaled, tables, parts, inner):
    each, both, points = tables[0].shape
    count = each * len(tables)
    width = both // 2

    def kernel(places_ref, scaled_ref, *refs):
        tables_refs, outs = refs[: len(tables)], refs[len(tables) : -3]
        held, kept, sems = refs[-3:]

        def fetch(j, ref, place):
            return pltpu.make_async_copy(ref.at[place], kept.at[j], sems.at[0, j])

        def leave(j, part):
            return pltpu.make_async_copy(held.at[j], outs[part].at[places_ref[1, j]], sems.at[1, j])

        for j in range(count):
            fetch(j, tables_refs[j // each], j % each).start()

        def body(j, carry):
            fetch(j, tables_refs[0], 0).wait()
            weighted = (kept[j, width:, :].astype(jnp.float32) * scaled_ref[...]).astype(
                jnp.bfloat16
            )
            held[j] = lax.dot_general(
                kept[j, :width, :],
                weighted,
                (((1,), (1,)), ((), ())),
                preferred_element_type=jnp.float32,
            ).astype(jnp.bfloat16)
            for part in range(parts):

                @pl.when(places_ref[0, j] == part)
                def _():
                    leave(j, part).start()

            return carry

        lax.fori_loop(0, count, body, 0)
        for j in range(count):
            leave(j, 0).wait()

    return pl.pallas_call(
        kernel,
        out_shape=[pltpu.HBM((inner, width, width), jnp.bfloat16)] * parts,
        in_specs=[SCALARS, RESIDENT] + [IN_HBM] * len(tables),
        out_specs=[IN_HBM] * parts,
        scratch_shapes=[
            pltpu.VMEM((count, width, width), jnp.bfloat16),
            pltpu.VMEM((count, both, points), jnp.bfloat16),
            pltpu.SemaphoreType.DMA((2, count)),
        ],
        compiler_params=params(52),
        name="integrate",
    )(places, scaled, *tables)


def add_up(bricks, numbers, parts, place, own_count, dtype):
    _, rows, cols = parts[0].shape
    count = len(parts)

    def kernel(bricks_ref, numbers_ref, *refs):
        parts_refs, (out_ref, held, total, sems) = refs[:count], refs[count:]

        def fetch(s):
            return pltpu.make_async_copy(parts_refs[s].at[place], held.at[s], sems.at[s])

        for s in range(count):

            @pl.when(numbers_ref[bricks_ref[s], place] >= 0)
            def _():
                fetch(s).start()

        total[...] = jnp.zeros_like(total)
        for s in range(count):
            target = numbers_ref[bricks_ref[s], place]

            @pl.when(target >= 0)
            def _():
                fetch(s).wait()
                total[target] += held[s].astype(jnp.float32)

        out_ref[...] = total[...].astype(dtype)

    return pl.pallas_call(
        kernel,
        out_shape=jax.ShapeDtypeStruct((own_count, rows, cols), dtype),
        in_specs=[SCALARS, SCALARS] + [IN_HBM] * count,
        out_specs=RESIDENT,
        scratch_shapes=[
            pltpu.VMEM((count, rows, cols), jnp.bfloat16),
            pltpu.VMEM((own_count, rows, cols), jnp.float32),
            pltpu.SemaphoreType.DMA((count,)),
        ],
        compiler_params=params(8),
        name="add_up",
    )(bricks, numbers, *parts)


def ends(block, dim, width):
    size = block.shape[dim]
    return (
        lax.slice_in_dim(block, 0, width, axis=dim),
        lax.slice_in_dim(block, size - width, size, axis=dim),
    )


def extended_ring(block, axis, dim, width):
    count = lax.axis_size(axis)
    low, high = ends(block, dim, width)
    forward = [(i, (i + 1) % count) for i in range(count)]
    backward = [(target, source) for source, target in forward]
    below = lax.ppermute(high, axis, forward)
    above = lax.ppermute(low, axis, backward)
    return jnp.concatenate([below, block, above], axis=dim)


def extended_pairs(block, axis, dim, width):
    count = size_of(axis)
    odd = lax.axis_index(axis) % 2 == 1
    low, high = ends(block, dim, width)
    within = [(i, i ^ 1) for i in range(count)]
    between = [(i, (i + 1) % count if i % 2 else (i - 1) % count) for i in range(count)]
    far = lax.ppermute(jnp.where(odd, high, low), axis, between)
    near = lax.ppermute(jnp.where(odd, low, high), axis, within)
    below = jnp.where(odd, near, far)
    above = jnp.where(odd, far, near)
    return jnp.concatenate([below, block, above], axis=dim)


def middle(field, dim, width=1):
    return lax.slice_in_dim(field, width, field.shape[dim] - width, axis=dim)


def slope(field, dim):
    size = field.shape[dim]
    return (
        lax.slice_in_dim(field, 2, size, axis=dim) - lax.slice_in_dim(field, 0, size - 2, axis=dim)
    ) * 0.5


def slope_z(field):
    return (jnp.roll(field, -1, 2) - jnp.roll(field, 1, 2)) * 0.5


def potential_of(padded):
    grad_x = middle(slope(padded, 0), 1)
    grad_y = middle(slope(padded, 1), 0)
    centre = middle(middle(padded, 0), 1)
    grad_z = slope_z(centre)
    sigma = grad_x * grad_x + grad_y * grad_y + grad_z * grad_z
    factor = 2.0 * GRAD_WEIGHT / (1.0 + sigma)
    flux_z = middle(middle(factor * grad_z, 0), 1)
    diverge = (
        middle(slope(factor * grad_x, 0), 1) + middle(slope(factor * grad_y, 1), 0) + slope_z(flux_z)
    )
    density = middle(middle(centre, 0), 1)
    return density / jnp.sqrt(1.0 + density * density) - diverge


def size_of(axes):
    return math.prod(lax.axis_size(axis) for axis in axes)


def moved(value, step, other, along):
    nx, ny, nc = (lax.axis_size(axis) for axis in BRICK)
    pairs = []
    for x in range(nx):
        for y in range(ny):
            for c in range(nc):
                core = (c + 1) % nc if other else c
                to_x, to_y = (x, (y + step) % ny) if along(c, core) else ((x + step) % nx, y)
                pairs.append(((x * ny + y) * nc + c, (to_x * ny + to_y) * nc + core))
    return lax.ppermute(value, BRICK, pairs)


def turns(side):
    far = [(o, k) for k in range(side) if k not in (0, 1, side - 1) for o in (0, 1)]
    return [(1, 0), (0, side - 1), (0, 1)] + far + [(1, 1), (1, side - 1)]


def order(side):
    return [side // 2] + [k for k in range(side) if k not in (side // 2, 0)]


def find(owners, ids, wanted):
    hit = owners[:, None, :] == wanted[None, :, None]
    return jnp.max(jnp.where(hit, ids[:, None, :], -1), axis=-1).astype(jnp.int32)


def local(store, crossing, phi, rows_index, cols_index):
    nx, ny, nc = (lax.axis_size(axis) for axis in BRICK)
    x, y, c = (lax.axis_index(axis) for axis in BRICK)
    position = (x * ny + y) * nc + c
    own_count, width = store.shape[0], store.shape[1]
    size_x, size_y, size_z, functions = phi.shape
    points = size_x * size_y * size_z
    owners = crossing // own_count
    ids = crossing % own_count
    slots = lax.dynamic_index_in_dim(owners, position, 0, keepdims=False)
    side = nx
    steps = jnp.arange(side)

    stores = [store] + [None] * (side - 1)
    for step in order(side):
        stores[step] = moved(store, step, False, lambda c, to: c == 1)
    table = phi.reshape(points, functions).T
    index = jnp.concatenate([rows_index[0], cols_index[0]], axis=1)[:, None, :]
    each = index.shape[0] // GATHERS
    pieces = [index[i : i + each] for i in range(0, index.shape[0], each)]
    ahead = jnp.where(c == 0, x * ny + (y + steps) % ny, ((x + steps) % nx) * ny + y) * nc
    served = jnp.concatenate([ahead + c, ahead + (1 - c)]).astype(jnp.int32)
    source = jnp.where(c == 0, ((x - steps) % nx) * ny + y, x * ny + (y - steps) % ny) * nc + c
    blocks = list(select_blocks(served, find(owners, ids, source), stores))
    *pieces[1:], blocks[side] = lax.optimization_barrier((*pieces[1:], blocks[side]))
    tables = [gather_tables(piece, table) for piece in pieces]
    for other, step in turns(side):
        i = other * side + step
        blocks[i] = moved(blocks[i], step, bool(other), lambda c, to: c == 0)
    to_x, rest = slots // (ny * nc), slots % (ny * nc)
    to_y, to_c = rest // nc, rest % nc
    behind_x, behind_y = (x - to_x) % nx, (y - to_y) % ny
    last = jnp.where(to_c == 0, behind_y, behind_x) + jnp.where(to_c == c, 0, side)
    places = jnp.stack([last, jnp.where(to_c == 0, behind_x, behind_y)]).astype(jnp.int32)
    layers = collocate(places, blocks, tables)
    density = jnp.sum(layers, axis=0).reshape(size_x, size_y, size_z)
    padded = extended_pairs(extended_ring(density, "grp", 0, 2), BRICK, 1, 2)
    scaled = potential_of(padded).reshape(1, points) * (1.0 / math.sqrt(points))

    ahead_x, ahead_y = (to_x - x) % nx, (to_y - y) % ny
    first = jnp.where(to_c == 0, ahead_y, ahead_x)
    second = jnp.where(to_c == 0, ahead_x, ahead_y)
    places = jnp.stack([first + jnp.where(to_c == c, 0, side), second]).astype(jnp.int32)
    parts = list(integrate(places, scaled, tables, 2 * side, side))
    for other, step in turns(side):
        i = other * side + step
        parts[i] = moved(parts[i], step, bool(other), lambda c, to: to == 0)
    behind = jnp.where(c == 0, x * ny + (y - steps) % ny, ((x - steps) % nx) * ny + y) * nc
    sources = jnp.concatenate([behind + c, behind + (1 - c)]).astype(jnp.int32)
    wanted = jnp.where(c == 0, ((x + steps) % nx) * ny + y, x * ny + (y + steps) % ny) * nc + c
    numbers = find(owners, ids, wanted)
    total = []
    for step in order(side):
        summed = add_up(sources, numbers, parts, step, own_count, jnp.bfloat16)
        total.append(moved(summed, step, False, lambda c, to: c == 1))
    own = add_up(sources, numbers, parts, 0, own_count, jnp.float32)
    for piece in total:
        own = own + piece.astype(jnp.float32)
    return own


def solution(mesh):
    groups, bricks = mesh.shape["grp"], mesh.shape["brick"]
    side = math.isqrt(bricks // 2)
    split = Mesh(mesh.devices.reshape(groups, side, bricks // (2 * side), 2), ("grp",) + BRICK)
    whole = ("grp",) + BRICK
    in_specs = (
        P(whole, None, None),
        P("grp", None),
        P("grp", BRICK, None, None),
        P(whole, None, None),
        P(whole, None, None),
    )
    return jax.shard_map(
        local, mesh=split, in_specs=in_specs, out_specs=P(whole, None, None), check_vma=False
    )
```

```python
import math

import jax
import jax.numpy as jnp
from jax import lax
from jax.experimental import pallas as pl
from jax.experimental.pallas import tpu as pltpu
from jax.sharding import Mesh
from jax.sharding import PartitionSpec as P

GRAD_WEIGHT = 0.5
GATHERS = 4
BRICK = ("x", "y", "core")
MIB = 1024 * 1024


RESIDENT = pl.BlockSpec(memory_space=pltpu.VMEM)
IN_HBM = pl.BlockSpec(memory_space=pltpu.HBM)
SCALARS = pl.BlockSpec(memory_space=pltpu.SMEM)


def params(mib):
    return pltpu.CompilerParams(vmem_limit_bytes=mib * MIB)


def select_blocks(bricks, numbers, stores):
    inner, parts = len(stores), bricks.shape[0]
    block = stores[0].shape[1:]

    def kernel(bricks_ref, numbers_ref, *refs):
        ins, outs, sems = refs[:inner], refs[inner:-1], refs[-1]
        places = [(p, d) for p in range(parts) for d in range(inner)]

        def copy(p, d):
            number = jnp.maximum(numbers_ref[bricks_ref[p], d], 0)
            return pltpu.make_async_copy(ins[d].at[number], outs[p].at[d], sems.at[p, d])

        for p, d in places:

            @pl.when(numbers_ref[bricks_ref[p], d] >= 0)
            def _():
                copy(p, d).start()

        for p, d in places:

            @pl.when(numbers_ref[bricks_ref[p], d] >= 0)
            def _():
                copy(p, d).wait()

    return pl.pallas_call(
        kernel,
        out_shape=[pltpu.HBM((inner,) + block, stores[0].dtype)] * parts,
        in_specs=[SCALARS, SCALARS] + [IN_HBM] * inner,
        out_specs=[IN_HBM] * parts,
        scratch_shapes=[pltpu.SemaphoreType.DMA((parts, inner))],
        compiler_params=params(4),
        name="select_blocks",
    )(bricks, numbers, *stores)


def gather_tables(index, table):
    count, _, width = index.shape
    functions, points = table.shape
    lanes = 128

    def kernel(index_ref, table_ref, out_ref):
        pieces = []
        for start in range(0, width, lanes):
            row = index_ref[0, :, start : start + lanes]
            column = jnp.broadcast_to(row, (lanes, lanes)).T
            hot = [
                jnp.where(
                    column == lax.broadcasted_iota(jnp.int32, (lanes, lanes), 1) + f, 1.0, 0.0
                ).astype(jnp.bfloat16)
                for f in range(0, functions, lanes)
            ]
            pieces.append(jnp.concatenate(hot, axis=1))
        onehot = jnp.concatenate(pieces, axis=0)
        out_ref[0] = jnp.dot(
            onehot, table_ref[...], preferred_element_type=jnp.float32
        ).astype(jnp.bfloat16)

    return pl.pallas_call(
        kernel,
        out_shape=pltpu.HBM((count, width, points), jnp.bfloat16),
        grid=(count,),
        in_specs=[
            pl.BlockSpec((1, 1, width), lambda i: (i, 0, 0)),
            pl.BlockSpec((functions, points), lambda i: (0, 0)),
        ],
        out_specs=pl.BlockSpec((1, width, points), lambda i: (i, 0, 0)),
        compiler_params=params(24),
        cost_estimate=pl.CostEstimate(
            flops=2 * count * width * functions * points,
            bytes_accessed=2 * count * width * points,
            transcendentals=0,
        ),
        name="gather_tables",
    )(index, table)


def collocate(places, blocks, tables):
    each, both, points = tables[0].shape
    count = each * len(tables)
    width = both // 2
    parts = len(blocks)

    def kernel(places_ref, *refs):
        blocks_refs, tables_refs = refs[:parts], refs[parts:-4]
        out_ref, held, kept, sems = refs[-4:]

        def fetch_block(j, part):
            return pltpu.make_async_copy(
                blocks_refs[part].at[places_ref[1, j]], held.at[j], sems.at[0, j]
            )

        def fetch_table(j, ref, place):
            return pltpu.make_async_copy(ref.at[place], kept.at[j], sems.at[1, j])

        for j in range(count):
            for part in range(parts):

                @pl.when(places_ref[0, j] == part)
                def _():
                    fetch_block(j, part).start()

            fetch_table(j, tables_refs[j // each], j % each).start()
        out_ref[...] = jnp.zeros_like(out_ref)

        def body(j, carry):
            fetch_block(j, 0).wait()
            fetch_table(j, tables_refs[0], 0).wait()
            product = jnp.dot(held[j], kept[j, width:, :], preferred_element_type=jnp.float32)
            term = kept[j, :width, :].astype(jnp.float32) * product
            out_ref[...] += jnp.sum(term.reshape(width // 8, 8, points), axis=0)
            return carry

        lax.fori_loop(0, count, body, 0)

    return pl.pallas_call(
        kernel,
        out_shape=jax.ShapeDtypeStruct((8, points), jnp.float32),
        in_specs=[SCALARS] + [IN_HBM] * (parts + len(tables)),
        out_specs=RESIDENT,
        scratch_shapes=[
            pltpu.VMEM((count, width, width), jnp.bfloat16),
            pltpu.VMEM((count, both, points), jnp.bfloat16),
            pltpu.SemaphoreType.DMA((2, count)),
        ],
        compiler_params=params(52),
        name="collocate",
    )(places, *blocks, *tables)


def integrate(places, scaled, tables, parts, inner):
    each, both, points = tables[0].shape
    count = each * len(tables)
    width = both // 2

    def kernel(places_ref, scaled_ref, *refs):
        tables_refs, outs = refs[: len(tables)], refs[len(tables) : -3]
        held, kept, sems = refs[-3:]

        def fetch(j, ref, place):
            return pltpu.make_async_copy(ref.at[place], kept.at[j], sems.at[0, j])

        def leave(j, part):
            return pltpu.make_async_copy(held.at[j], outs[part].at[places_ref[1, j]], sems.at[1, j])

        for j in range(count):
            fetch(j, tables_refs[j // each], j % each).start()

        def body(j, carry):
            fetch(j, tables_refs[0], 0).wait()
            weighted = (kept[j, width:, :].astype(jnp.float32) * scaled_ref[...]).astype(
                jnp.bfloat16
            )
            held[j] = lax.dot_general(
                kept[j, :width, :],
                weighted,
                (((1,), (1,)), ((), ())),
                preferred_element_type=jnp.float32,
            ).astype(jnp.bfloat16)
            for part in range(parts):

                @pl.when(places_ref[0, j] == part)
                def _():
                    leave(j, part).start()

            return carry

        lax.fori_loop(0, count, body, 0)
        for j in range(count):
            leave(j, 0).wait()

    return pl.pallas_call(
        kernel,
        out_shape=[pltpu.HBM((inner, width, width), jnp.bfloat16)] * parts,
        in_specs=[SCALARS, RESIDENT] + [IN_HBM] * len(tables),
        out_specs=[IN_HBM] * parts,
        scratch_shapes=[
            pltpu.VMEM((count, width, width), jnp.bfloat16),
            pltpu.VMEM((count, both, points), jnp.bfloat16),
            pltpu.SemaphoreType.DMA((2, count)),
        ],
        compiler_params=params(52),
        name="integrate",
    )(places, scaled, *tables)


def add_up(bricks, numbers, parts, place, own_count, dtype):
    _, rows, cols = parts[0].shape
    count = len(parts)

    def kernel(bricks_ref, numbers_ref, *refs):
        parts_refs, (out_ref, held, total, sems) = refs[:count], refs[count:]

        def fetch(s):
            return pltpu.make_async_copy(parts_refs[s].at[place], held.at[s], sems.at[s])

        for s in range(count):

            @pl.when(numbers_ref[bricks_ref[s], place] >= 0)
            def _():
                fetch(s).start()

        total[...] = jnp.zeros_like(total)
        for s in range(count):
            target = numbers_ref[bricks_ref[s], place]

            @pl.when(target >= 0)
            def _():
                fetch(s).wait()
                total[target] += held[s].astype(jnp.float32)

        out_ref[...] = total[...].astype(dtype)

    return pl.pallas_call(
        kernel,
        out_shape=jax.ShapeDtypeStruct((own_count, rows, cols), dtype),
        in_specs=[SCALARS, SCALARS] + [IN_HBM] * count,
        out_specs=RESIDENT,
        scratch_shapes=[
            pltpu.VMEM((count, rows, cols), jnp.bfloat16),
            pltpu.VMEM((own_count, rows, cols), jnp.float32),
            pltpu.SemaphoreType.DMA((count,)),
        ],
        compiler_params=params(8),
        name="add_up",
    )(bricks, numbers, *parts)


def ends(block, dim, width):
    size = block.shape[dim]
    return (
        lax.slice_in_dim(block, 0, width, axis=dim),
        lax.slice_in_dim(block, size - width, size, axis=dim),
    )


def extended_ring(block, axis, dim, width):
    count = lax.axis_size(axis)
    low, high = ends(block, dim, width)
    forward = [(i, (i + 1) % count) for i in range(count)]
    backward = [(target, source) for source, target in forward]
    below = lax.ppermute(high, axis, forward)
    above = lax.ppermute(low, axis, backward)
    return jnp.concatenate([below, block, above], axis=dim)


def extended_pairs(block, axis, dim, width):
    count = size_of(axis)
    odd = lax.axis_index(axis) % 2 == 1
    low, high = ends(block, dim, width)
    within = [(i, i ^ 1) for i in range(count)]
    between = [(i, (i + 1) % count if i % 2 else (i - 1) % count) for i in range(count)]
    far = lax.ppermute(jnp.where(odd, high, low), axis, between)
    near = lax.ppermute(jnp.where(odd, low, high), axis, within)
    below = jnp.where(odd, near, far)
    above = jnp.where(odd, far, near)
    return jnp.concatenate([below, block, above], axis=dim)


def middle(field, dim, width=1):
    return lax.slice_in_dim(field, width, field.shape[dim] - width, axis=dim)


def slope(field, dim):
    size = field.shape[dim]
    return (
        lax.slice_in_dim(field, 2, size, axis=dim) - lax.slice_in_dim(field, 0, size - 2, axis=dim)
    ) * 0.5


def slope_z(field):
    return (jnp.roll(field, -1, 2) - jnp.roll(field, 1, 2)) * 0.5


def potential_of(padded):
    grad_x = middle(slope(padded, 0), 1)
    grad_y = middle(slope(padded, 1), 0)
    centre = middle(middle(padded, 0), 1)
    grad_z = slope_z(centre)
    sigma = grad_x * grad_x + grad_y * grad_y + grad_z * grad_z
    factor = 2.0 * GRAD_WEIGHT / (1.0 + sigma)
    flux_z = middle(middle(factor * grad_z, 0), 1)
    diverge = (
        middle(slope(factor * grad_x, 0), 1) + middle(slope(factor * grad_y, 1), 0) + slope_z(flux_z)
    )
    density = middle(middle(centre, 0), 1)
    return density / jnp.sqrt(1.0 + density * density) - diverge


def size_of(axes):
    return math.prod(lax.axis_size(axis) for axis in axes)


def moved(value, step, other, along):
    nx, ny, nc = (lax.axis_size(axis) for axis in BRICK)
    pairs = []
    for x in range(nx):
        for y in range(ny):
            for c in range(nc):
                core = (c + 1) % nc if other else c
                to_x, to_y = (x, (y + step) % ny) if along(c, core) else ((x + step) % nx, y)
                pairs.append(((x * ny + y) * nc + c, (to_x * ny + to_y) * nc + core))
    return lax.ppermute(value, BRICK, pairs)


def turns(side):
    far = [(o, k) for k in range(side) if k not in (0, 1, side - 1) for o in (0, 1)]
    return [(1, 0), (0, side - 1), (0, 1)] + far + [(1, 1), (1, side - 1)]


def order(side):
    return [side // 2] + [k for k in range(side) if k not in (side // 2, 0)]


def find(owners, ids, wanted):
    hit = owners[:, None, :] == wanted[None, :, None]
    return jnp.max(jnp.where(hit, ids[:, None, :], -1), axis=-1).astype(jnp.int32)


def local(store, crossing, phi, rows_index, cols_index):
    nx, ny, nc = (lax.axis_size(axis) for axis in BRICK)
    x, y, c = (lax.axis_index(axis) for axis in BRICK)
    position = (x * ny + y) * nc + c
    own_count, width = store.shape[0], store.shape[1]
    size_x, size_y, size_z, functions = phi.shape
    points = size_x * size_y * size_z
    owners = crossing // own_count
    ids = crossing % own_count
    slots = lax.dynamic_index_in_dim(owners, position, 0, keepdims=False)
    side = nx
    steps = jnp.arange(side)

    stores = [store] + [None] * (side - 1)
    for step in order(side):
        stores[step] = moved(store, step, False, lambda c, to: c == 1)
    table = phi.reshape(points, functions).T
    index = jnp.concatenate([rows_index[0], cols_index[0]], axis=1)[:, None, :]
    each = index.shape[0] // GATHERS
    pieces = [index[i : i + each] for i in range(0, index.shape[0], each)]
    ahead = jnp.where(c == 0, x * ny + (y + steps) % ny, ((x + steps) % nx) * ny + y) * nc
    served = jnp.concatenate([ahead + c, ahead + (1 - c)]).astype(jnp.int32)
    source = jnp.where(c == 0, ((x - steps) % nx) * ny + y, x * ny + (y - steps) % ny) * nc + c
    blocks = list(select_blocks(served, find(owners, ids, source), stores))
    *pieces[1:], blocks[side] = lax.optimization_barrier((*pieces[1:], blocks[side]))
    tables = [gather_tables(piece, table) for piece in pieces]
    for other, step in turns(side):
        i = other * side + step
        blocks[i] = moved(blocks[i], step, bool(other), lambda c, to: c == 0)
    to_x, rest = slots // (ny * nc), slots % (ny * nc)
    to_y, to_c = rest // nc, rest % nc
    behind_x, behind_y = (x - to_x) % nx, (y - to_y) % ny
    last = jnp.where(to_c == 0, behind_y, behind_x) + jnp.where(to_c == c, 0, side)
    places = jnp.stack([last, jnp.where(to_c == 0, behind_x, behind_y)]).astype(jnp.int32)
    layers = collocate(places, blocks, tables)
    density = jnp.sum(layers, axis=0).reshape(size_x, size_y, size_z)
    padded = extended_pairs(extended_ring(density, "grp", 0, 2), BRICK, 1, 2)
    scaled = potential_of(padded).reshape(1, points) * (1.0 / math.sqrt(points))

    ahead_x, ahead_y = (to_x - x) % nx, (to_y - y) % ny
    first = jnp.where(to_c == 0, ahead_y, ahead_x)
    second = jnp.where(to_c == 0, ahead_x, ahead_y)
    places = jnp.stack([first + jnp.where(to_c == c, 0, side), second]).astype(jnp.int32)
    parts = list(integrate(places, scaled, tables, 2 * side, side))
    for other, step in turns(side):
        i = other * side + step
        parts[i] = moved(parts[i], step, bool(other), lambda c, to: to == 0)
    behind = jnp.where(c == 0, x * ny + (y - steps) % ny, ((x - steps) % nx) * ny + y) * nc
    sources = jnp.concatenate([behind + c, behind + (1 - c)]).astype(jnp.int32)
    wanted = jnp.where(c == 0, ((x + steps) % nx) * ny + y, x * ny + (y + steps) % ny) * nc + c
    numbers = find(owners, ids, wanted)
    ranks = [0] + [other * side + step for other, step in turns(side)]
    parts = [parts[i] for i in ranks]
    sources = jnp.stack([sources[i] for i in ranks])
    total = []
    for step in order(side):
        summed = add_up(sources, numbers, parts, step, own_count, jnp.bfloat16)
        total.append(moved(summed, step, False, lambda c, to: c == 1))
    own = add_up(sources, numbers, parts, 0, own_count, jnp.float32)
    for piece in total:
        own = own + piece.astype(jnp.float32)
    return own


def solution(mesh):
    groups, bricks = mesh.shape["grp"], mesh.shape["brick"]
    side = math.isqrt(bricks // 2)
    split = Mesh(mesh.devices.reshape(groups, side, bricks // (2 * side), 2), ("grp",) + BRICK)
    whole = ("grp",) + BRICK
    in_specs = (
        P(whole, None, None),
        P("grp", None),
        P("grp", BRICK, None, None),
        P(whole, None, None),
        P(whole, None, None),
    )
    return jax.shard_map(
        local, mesh=split, in_specs=in_specs, out_specs=P(whole, None, None), check_vma=False
    )
```

```python
import math

import jax
import jax.numpy as jnp
from jax import lax
from jax.experimental import pallas as pl
from jax.experimental.pallas import tpu as pltpu
from jax.sharding import Mesh
from jax.sharding import PartitionSpec as P

GRAD_WEIGHT = 0.5
GATHERS = 4
BRICK = ("x", "y", "core")
MIB = 1024 * 1024


RESIDENT = pl.BlockSpec(memory_space=pltpu.VMEM)
IN_HBM = pl.BlockSpec(memory_space=pltpu.HBM)
SCALARS = pl.BlockSpec(memory_space=pltpu.SMEM)


def params(mib):
    return pltpu.CompilerParams(vmem_limit_bytes=mib * MIB)


def select_blocks(bricks, numbers, stores):
    inner, parts = len(stores), bricks.shape[0]
    block = stores[0].shape[1:]

    def kernel(bricks_ref, numbers_ref, *refs):
        ins, outs, sems = refs[:inner], refs[inner:-1], refs[-1]
        places = [(p, d) for p in range(parts) for d in range(inner)]

        def copy(p, d):
            number = jnp.maximum(numbers_ref[bricks_ref[p], d], 0)
            return pltpu.make_async_copy(ins[d].at[number], outs[p].at[d], sems.at[p, d])

        for p, d in places:

            @pl.when(numbers_ref[bricks_ref[p], d] >= 0)
            def _():
                copy(p, d).start()

        for p, d in places:

            @pl.when(numbers_ref[bricks_ref[p], d] >= 0)
            def _():
                copy(p, d).wait()

    return pl.pallas_call(
        kernel,
        out_shape=[pltpu.HBM((inner,) + block, stores[0].dtype)] * parts,
        in_specs=[SCALARS, SCALARS] + [IN_HBM] * inner,
        out_specs=[IN_HBM] * parts,
        scratch_shapes=[pltpu.SemaphoreType.DMA((parts, inner))],
        compiler_params=params(4),
        name="select_blocks",
    )(bricks, numbers, *stores)


def gather_tables(index, table):
    count, _, width = index.shape
    functions, points = table.shape
    lanes = 128

    def kernel(index_ref, table_ref, out_ref):
        pieces = []
        for start in range(0, width, lanes):
            row = index_ref[0, :, start : start + lanes]
            column = jnp.broadcast_to(row, (lanes, lanes)).T
            hot = [
                jnp.where(
                    column == lax.broadcasted_iota(jnp.int32, (lanes, lanes), 1) + f, 1.0, 0.0
                ).astype(jnp.bfloat16)
                for f in range(0, functions, lanes)
            ]
            pieces.append(jnp.concatenate(hot, axis=1))
        onehot = jnp.concatenate(pieces, axis=0)
        out_ref[0] = jnp.dot(
            onehot, table_ref[...], preferred_element_type=jnp.float32
        ).astype(jnp.bfloat16)

    return pl.pallas_call(
        kernel,
        out_shape=pltpu.HBM((count, width, points), jnp.bfloat16),
        grid=(count,),
        in_specs=[
            pl.BlockSpec((1, 1, width), lambda i: (i, 0, 0)),
            pl.BlockSpec((functions, points), lambda i: (0, 0)),
        ],
        out_specs=pl.BlockSpec((1, width, points), lambda i: (i, 0, 0)),
        compiler_params=params(24),
        cost_estimate=pl.CostEstimate(
            flops=2 * count * width * functions * points,
            bytes_accessed=2 * count * width * points,
            transcendentals=0,
        ),
        name="gather_tables",
    )(index, table)


def collocate(places, blocks, tables):
    each, both, points = tables[0].shape
    count = each * len(tables)
    width = both // 2
    parts = len(blocks)

    def kernel(places_ref, *refs):
        blocks_refs, tables_refs = refs[:parts], refs[parts:-4]
        out_ref, held, kept, sems = refs[-4:]

        def fetch_block(j, part):
            return pltpu.make_async_copy(
                blocks_refs[part].at[places_ref[1, j]], held.at[j], sems.at[0, j]
            )

        def fetch_table(j, ref, place):
            return pltpu.make_async_copy(ref.at[place], kept.at[j], sems.at[1, j])

        for j in range(count):
            for part in range(parts):

                @pl.when(places_ref[0, j] == part)
                def _():
                    fetch_block(j, part).start()

            fetch_table(j, tables_refs[j // each], j % each).start()
        out_ref[...] = jnp.zeros_like(out_ref)

        def body(j, carry):
            fetch_block(j, 0).wait()
            fetch_table(j, tables_refs[0], 0).wait()
            product = jnp.dot(held[j], kept[j, width:, :], preferred_element_type=jnp.float32)
            term = kept[j, :width, :].astype(jnp.float32) * product
            out_ref[...] += jnp.sum(term.reshape(width // 8, 8, points), axis=0)
            return carry

        lax.fori_loop(0, count, body, 0)

    return pl.pallas_call(
        kernel,
        out_shape=jax.ShapeDtypeStruct((8, points), jnp.float32),
        in_specs=[SCALARS] + [IN_HBM] * (parts + len(tables)),
        out_specs=RESIDENT,
        scratch_shapes=[
            pltpu.VMEM((count, width, width), jnp.bfloat16),
            pltpu.VMEM((count, both, points), jnp.bfloat16),
            pltpu.SemaphoreType.DMA((2, count)),
        ],
        compiler_params=params(52),
        name="collocate",
    )(places, *blocks, *tables)


def integrate(places, scaled, tables, parts, inner):
    each, both, points = tables[0].shape
    count = each * len(tables)
    width = both // 2

    def kernel(places_ref, scaled_ref, *refs):
        tables_refs, outs = refs[: len(tables)], refs[len(tables) : -3]
        held, kept, sems = refs[-3:]

        def fetch(j, ref, place):
            return pltpu.make_async_copy(ref.at[place], kept.at[j], sems.at[0, j])

        def leave(j, part):
            return pltpu.make_async_copy(held.at[j], outs[part].at[places_ref[1, j]], sems.at[1, j])

        for j in range(count):
            fetch(j, tables_refs[j // each], j % each).start()

        def body(j, carry):
            fetch(j, tables_refs[0], 0).wait()
            weighted = (kept[j, width:, :].astype(jnp.float32) * scaled_ref[...]).astype(
                jnp.bfloat16
            )
            held[j] = lax.dot_general(
                kept[j, :width, :],
                weighted,
                (((1,), (1,)), ((), ())),
                preferred_element_type=jnp.float32,
            ).astype(jnp.bfloat16)
            for part in range(parts):

                @pl.when(places_ref[0, j] == part)
                def _():
                    leave(j, part).start()

            return carry

        lax.fori_loop(0, count, body, 0)
        for j in range(count):
            leave(j, 0).wait()

    return pl.pallas_call(
        kernel,
        out_shape=[pltpu.HBM((inner, width, width), jnp.bfloat16)] * parts,
        in_specs=[SCALARS, RESIDENT] + [IN_HBM] * len(tables),
        out_specs=[IN_HBM] * parts,
        scratch_shapes=[
            pltpu.VMEM((count, width, width), jnp.bfloat16),
            pltpu.VMEM((count, both, points), jnp.bfloat16),
            pltpu.SemaphoreType.DMA((2, count)),
        ],
        compiler_params=params(52),
        name="integrate",
    )(places, scaled, *tables)


def add_up(bricks, numbers, parts, place, own_count, dtype):
    _, rows, cols = parts[0].shape
    count = len(parts)

    def kernel(bricks_ref, numbers_ref, *refs):
        parts_refs, (out_ref, held, total, sems) = refs[:count], refs[count:]

        def fetch(s):
            return pltpu.make_async_copy(parts_refs[s].at[place], held.at[s], sems.at[s])

        for s in range(count):

            @pl.when(numbers_ref[bricks_ref[s], place] >= 0)
            def _():
                fetch(s).start()

        total[...] = jnp.zeros_like(total)
        for s in range(count):
            target = numbers_ref[bricks_ref[s], place]

            @pl.when(target >= 0)
            def _():
                fetch(s).wait()
                total[target] += held[s].astype(jnp.float32)

        out_ref[...] = total[...].astype(dtype)

    return pl.pallas_call(
        kernel,
        out_shape=jax.ShapeDtypeStruct((own_count, rows, cols), dtype),
        in_specs=[SCALARS, SCALARS] + [IN_HBM] * count,
        out_specs=RESIDENT,
        scratch_shapes=[
            pltpu.VMEM((count, rows, cols), jnp.bfloat16),
            pltpu.VMEM((own_count, rows, cols), jnp.float32),
            pltpu.SemaphoreType.DMA((count,)),
        ],
        compiler_params=params(8),
        name="add_up",
    )(bricks, numbers, *parts)


def ends(block, dim, width):
    size = block.shape[dim]
    return (
        lax.slice_in_dim(block, 0, width, axis=dim),
        lax.slice_in_dim(block, size - width, size, axis=dim),
    )


def extended_ring(block, axis, dim, width):
    count = lax.axis_size(axis)
    low, high = ends(block, dim, width)
    forward = [(i, (i + 1) % count) for i in range(count)]
    backward = [(target, source) for source, target in forward]
    below = lax.ppermute(high, axis, forward)
    above = lax.ppermute(low, axis, backward)
    return jnp.concatenate([below, block, above], axis=dim)


def extended_pairs(block, axis, dim, width):
    count = size_of(axis)
    odd = lax.axis_index(axis) % 2 == 1
    low, high = ends(block, dim, width)
    within = [(i, i ^ 1) for i in range(count)]
    between = [(i, (i + 1) % count if i % 2 else (i - 1) % count) for i in range(count)]
    far = lax.ppermute(jnp.where(odd, high, low), axis, between)
    near = lax.ppermute(jnp.where(odd, low, high), axis, within)
    below = jnp.where(odd, near, far)
    above = jnp.where(odd, far, near)
    return jnp.concatenate([below, block, above], axis=dim)


def middle(field, dim, width=1):
    return lax.slice_in_dim(field, width, field.shape[dim] - width, axis=dim)


def slope(field, dim):
    size = field.shape[dim]
    return (
        lax.slice_in_dim(field, 2, size, axis=dim) - lax.slice_in_dim(field, 0, size - 2, axis=dim)
    ) * 0.5


def slope_z(field):
    return (jnp.roll(field, -1, 2) - jnp.roll(field, 1, 2)) * 0.5


def potential_of(padded):
    grad_x = middle(slope(padded, 0), 1)
    grad_y = middle(slope(padded, 1), 0)
    centre = middle(middle(padded, 0), 1)
    grad_z = slope_z(centre)
    sigma = grad_x * grad_x + grad_y * grad_y + grad_z * grad_z
    factor = 2.0 * GRAD_WEIGHT / (1.0 + sigma)
    flux_z = middle(middle(factor * grad_z, 0), 1)
    diverge = (
        middle(slope(factor * grad_x, 0), 1) + middle(slope(factor * grad_y, 1), 0) + slope_z(flux_z)
    )
    density = middle(middle(centre, 0), 1)
    return density / jnp.sqrt(1.0 + density * density) - diverge


def size_of(axes):
    return math.prod(lax.axis_size(axis) for axis in axes)


def moved(value, step, other, along):
    nx, ny, nc = (lax.axis_size(axis) for axis in BRICK)
    pairs = []
    for x in range(nx):
        for y in range(ny):
            for c in range(nc):
                core = (c + 1) % nc if other else c
                to_x, to_y = (x, (y + step) % ny) if along(c, core) else ((x + step) % nx, y)
                pairs.append(((x * ny + y) * nc + c, (to_x * ny + to_y) * nc + core))
    return lax.ppermute(value, BRICK, pairs)


def turns(side):
    far = [(o, k) for k in range(side) if k not in (0, 1, side - 1) for o in (0, 1)]
    return [(1, 0), (0, side - 1), (0, 1)] + far + [(1, 1), (1, side - 1)]


def order(side):
    return [side // 2] + [k for k in range(side) if k not in (side // 2, 0)]


def find(owners, ids, wanted):
    hit = owners[:, None, :] == wanted[None, :, None]
    return jnp.max(jnp.where(hit, ids[:, None, :], -1), axis=-1).astype(jnp.int32)


def local(store, crossing, phi, rows_index, cols_index):
    nx, ny, nc = (lax.axis_size(axis) for axis in BRICK)
    x, y, c = (lax.axis_index(axis) for axis in BRICK)
    position = (x * ny + y) * nc + c
    own_count, width = store.shape[0], store.shape[1]
    size_x, size_y, size_z, functions = phi.shape
    points = size_x * size_y * size_z
    owners = crossing // own_count
    ids = crossing % own_count
    slots = lax.dynamic_index_in_dim(owners, position, 0, keepdims=False)
    side = nx
    steps = jnp.arange(side)

    stores = [store] + [None] * (side - 1)
    for step in order(side):
        stores[step] = moved(store, step, False, lambda c, to: c == 1)
    table = phi.reshape(points, functions).T
    index = jnp.concatenate([rows_index[0], cols_index[0]], axis=1)[:, None, :]
    each = index.shape[0] // GATHERS
    pieces = [index[i : i + each] for i in range(0, index.shape[0], each)]
    ahead = jnp.where(c == 0, x * ny + (y + steps) % ny, ((x + steps) % nx) * ny + y) * nc
    served = jnp.concatenate([ahead + c, ahead + (1 - c)]).astype(jnp.int32)
    source = jnp.where(c == 0, ((x - steps) % nx) * ny + y, x * ny + (y - steps) % ny) * nc + c
    blocks = list(select_blocks(served, find(owners, ids, source), stores))
    *pieces[1:], blocks[side] = lax.optimization_barrier((*pieces[1:], blocks[side]))
    tables = [gather_tables(piece, table) for piece in pieces]
    for other, step in turns(side):
        i = other * side + step
        blocks[i] = moved(blocks[i], step, bool(other), lambda c, to: c == 0)
    to_x, rest = slots // (ny * nc), slots % (ny * nc)
    to_y, to_c = rest // nc, rest % nc
    behind_x, behind_y = (x - to_x) % nx, (y - to_y) % ny
    last = jnp.where(to_c == 0, behind_y, behind_x) + jnp.where(to_c == c, 0, side)
    places = jnp.stack([last, jnp.where(to_c == 0, behind_x, behind_y)]).astype(jnp.int32)
    layers = collocate(places, blocks, tables)
    density = jnp.sum(layers, axis=0).reshape(size_x, size_y, size_z)
    padded = extended_pairs(extended_ring(density, "grp", 0, 2), BRICK, 1, 2)
    scaled = potential_of(padded).reshape(1, points) * (1.0 / math.sqrt(points))

    ahead_x, ahead_y = (to_x - x) % nx, (to_y - y) % ny
    first = jnp.where(to_c == 0, ahead_y, ahead_x)
    second = jnp.where(to_c == 0, ahead_x, ahead_y)
    places = jnp.stack([first + jnp.where(to_c == c, 0, side), second]).astype(jnp.int32)
    parts = list(integrate(places, scaled, tables, 2 * side, side))
    for other, step in turns(side):
        i = other * side + step
        parts[i] = moved(parts[i], step, bool(other), lambda c, to: to == 0)
    wanted = jnp.where(c == 0, ((x + steps) % nx) * ny + y, x * ny + (y + steps) % ny) * nc + c
    numbers = find(owners, ids, wanted)
    ranks = [0] + [other * side + step for other, step in turns(side)]
    parts = [parts[i] for i in ranks]
    back = jnp.array([i % side for i in ranks], jnp.int32)
    core = jnp.where(jnp.array([i >= side for i in ranks]), 1 - c, c)
    behind = jnp.where(c == 0, x * ny + (y - back) % ny, ((x - back) % nx) * ny + y)
    sources = (behind * nc + core).astype(jnp.int32)
    total = []
    for step in order(side):
        summed = add_up(sources, numbers, parts, step, own_count, jnp.bfloat16)
        total.append(moved(summed, step, False, lambda c, to: c == 1))
    own = add_up(sources, numbers, parts, 0, own_count, jnp.float32)
    for piece in total:
        own = own + piece.astype(jnp.float32)
    return own


def solution(mesh):
    groups, bricks = mesh.shape["grp"], mesh.shape["brick"]
    side = math.isqrt(bricks // 2)
    split = Mesh(mesh.devices.reshape(groups, side, bricks // (2 * side), 2), ("grp",) + BRICK)
    whole = ("grp",) + BRICK
    in_specs = (
        P(whole, None, None),
        P("grp", None),
        P("grp", BRICK, None, None),
        P(whole, None, None),
        P(whole, None, None),
    )
    return jax.shard_map(
        local, mesh=split, in_specs=in_specs, out_specs=P(whole, None, None), check_vma=False
    )
```
